768 devices in a mesh: section: 4 (over z_hi), row: 64 (over x, y, core), col: 3 (over z_lo).
Axes of the slice: x: 4, y: 8, z: 12 (z_hi: 4, z_lo: 3; z = z_hi * 3 + z_lo), core: 2. Of those that a mesh axis runs over, the one named last changes fastest.
Arguments:
- act_in: bfloat16 [4, 128, 12288], P('section', 'row', 'col'), may hold values from -6 to 6
- hid_in: bfloat16 [4, 128, 24576], P('section', None, 'row'), may hold values from -6 to 6
- grad_in: bfloat16 [4, 128, 12288], P('section', 'row', 'col'), may hold values from -6 to 6
- saved_in: bfloat16 [4, 128, 12288], P('section', 'row', 'col'), may hold values from -6 to 6
- saved_pre: bfloat16 [4, 128, 24576], P('section', None, 'row'), may hold values from -6 to 6
- weights: bfloat16 [4, 12288, 24576], P('section', 'col', 'row'), may hold values from -0.0546875 to 0.0546875
- norm_gain: float32 [2, 12288], P(None, 'col'), may hold values from 0.25 to 1.75
- norm_bias: float32 [2, 12288], P(None, 'col'), may hold values from -0.5 to 0.5
Outputs:
- act_out: bfloat16 [4, 128, 12288], P('section', 'row', 'col')
- hid_out: bfloat16 [4, 128, 24576], P('section', None, 'row')
- grad_out: bfloat16 [4, 128, 12288], P('section', 'row', 'col')
The draws below stay inside these ranges and needn't reach their ends.
All inputs are finite; a program needn't handle non-finite values.
Results may differ from the reference program's by a relative error of at most 0.0035.
Values may be sent and summed in bfloat16 or wider, within the bound.
No kernel may reach another device: no remote copies, remote signals or barrier semaphores. Data moves between devices by JAX's collectives and lax.ppermute only.
A program may use at most 32 MiB of HBM per device.

```python
import jax
import jax.numpy as jnp
from jax import lax

D = 12288
FF = 24576
TOKENS = 128
LAYERS = 2
N_SECTION = 4


def shard_levels(own_key, extent, cuts, least, top_value):
    def one(position, shards_of):
        heights = jax.random.uniform(jax.random.fold_in(jax.random.fold_in(own_key, 6), position), (shards_of,), jnp.float32, least / len(cuts), top_value / len(cuts))
        return jnp.repeat(jnp.exp(heights), extent[position] // shards_of).reshape((-1,) + (1,) * (len(extent) - position - 1))

    level = one(*cuts[0])
    for cut in cuts[1:]:
        level = level * one(*cut)
    return level


def normal_values(own_key, shape, width, limit, pieces=(), held_as=jnp.bfloat16):
    values = jax.random.normal(own_key, shape, jnp.float32) * width
    if len(pieces) > 0:
        values = shard_levels(own_key, shape, pieces, -0.22, 0.18) * values
    return jnp.clip(values, min=-limit, max=limit).astype(held_as)


def setup_inputs(seed: int = 0) -> dict:
    seeds = jax.random.split(jax.random.key(seed), 9)
    act_in = normal_values(seeds[0], (N_SECTION, TOKENS, D), 1.0, 6.0, ((0, 4), (1, 64), (2, 3)))
    hid_in = normal_values(seeds[1], (N_SECTION, TOKENS, FF), 1.0, 6.0, ((0, 4), (2, 64)))
    grad_in = normal_values(seeds[2], (N_SECTION, TOKENS, D), 1.0, 6.0, ((0, 4), (1, 64), (2, 3)))
    saved_in = normal_values(seeds[3], (N_SECTION, TOKENS, D), 1.0, 6.0, ((0, 4), (1, 64), (2, 3)))
    saved_pre = normal_values(seeds[4], (N_SECTION, TOKENS, FF), 1.5, 6.0, ((0, 4), (2, 64)))
    weights = normal_values(seeds[5], (N_SECTION, D, FF), D ** -0.5, 0.0546875, ((0, 4), (1, 3), (2, 64)))
    norm_gain = jnp.clip(1.0 + 0.15 * jax.random.normal(seeds[6], (LAYERS, D), jnp.float32), 0.25, 1.75)
    norm_bias = jnp.clip(jax.random.uniform(seeds[7], (LAYERS, D), jnp.float32, -0.5, 0.5) * shard_levels(seeds[7], (LAYERS, D), ((1, 3),), -0.4, 0.0), -0.5, 0.5)
    return dict(act_in=act_in, hid_in=hid_in, grad_in=grad_in, saved_in=saved_in, saved_pre=saved_pre, weights=weights, norm_gain=norm_gain, norm_bias=norm_bias)


epsilon = 1e-05

def normalized(values):
    floats = values.astype(jnp.float32)
    average = lax.optimization_barrier(jnp.sum(floats, axis=-1, keepdims=True)) / D
    squares = lax.optimization_barrier(jnp.sum(floats * floats, axis=-1, keepdims=True)) / D
    inverse_scale = lax.rsqrt(squares - average * average + epsilon)
    return ((floats - average) * inverse_scale, inverse_scale)

def gelu_slope(preact, upstream):
    return jax.vjp(lambda value: jax.nn.gelu(value, approximate=True), preact)[1](upstream)[0]

def reference(act_in, hid_in, grad_in, saved_in, saved_pre, weights, norm_gain, norm_bias):
    act_list = [None] * N_SECTION
    hid_list = [None] * N_SECTION
    grad_list = [None] * N_SECTION
    for section_index in range(N_SECTION):
        weight = weights[section_index]
        if section_index % 2 == 0:
            layer = section_index // 2
            gain = norm_gain[layer]
            centred, unused_scale = normalized(act_in[section_index])
            normed = (centred * gain + norm_bias[layer]).astype(jnp.bfloat16)
            preact = jnp.dot(normed, weight, preferred_element_type=jnp.float32)
            hidden_out = jax.nn.gelu(preact, approximate=True).astype(jnp.bfloat16)
            forward = act_in[section_index]
            saved_hat, saved_scale = normalized(saved_in[section_index])
            slope = gelu_slope(saved_pre[section_index].astype(jnp.float32), hid_in[section_index].astype(jnp.float32)).astype(jnp.bfloat16)
            back_rows = jnp.dot(slope, weight.T, preferred_element_type=jnp.float32)
            scaled = back_rows * gain
            first_mean = lax.optimization_barrier(jnp.sum(scaled, axis=-1, keepdims=True)) / D
            second_mean = lax.optimization_barrier(jnp.sum(scaled * saved_hat, axis=-1, keepdims=True)) / D
            backward = (grad_in[section_index].astype(jnp.float32) + saved_scale * (scaled - first_mean - saved_hat * second_mean)).astype(jnp.bfloat16)
            hid_list[section_index + 1] = hidden_out
        else:
            term = jnp.dot(hid_in[section_index], weight.T, preferred_element_type=jnp.float32)
            forward = (act_in[section_index].astype(jnp.float32) + term).astype(jnp.bfloat16)
            hidden_out = jnp.dot(grad_in[section_index], weight, preferred_element_type=jnp.float32).astype(jnp.bfloat16)
            backward = grad_in[section_index]
            hid_list[section_index - 1] = hidden_out
        act_list[(section_index + 1) % N_SECTION] = forward
        grad_list[(section_index - 1) % N_SECTION] = backward
    return (jnp.stack(act_list), jnp.stack(hid_list), jnp.stack(grad_list))
```

```python
import jax
import jax.numpy as jnp
from jax import lax
from jax.sharding import Mesh, PartitionSpec as P

D = 12288
epsilon = 1e-05

LAYER_AXIS, HALF, COLS = "layer", "half", "cols"
PLANE = ("px", "py")
CORE = "core"
ROWS = PLANE + (CORE,)
SECTION = (LAYER_AXIS, HALF)


def boundary(values, offset):
    return lax.ppermute(values, SECTION, [(i, (i + offset) % 4) for i in range(4)])


def statistics(total, squares):
    average = total / D
    inverse_scale = lax.rsqrt(squares / D - average * average + epsilon)
    return (average[:, None], inverse_scale[:, None])


def gelu_slope(preact, upstream):
    return jax.vjp(lambda value: jax.nn.gelu(value, approximate=True), preact)[1](upstream)[0]


def per_device(act_in, hid_in, grad_in, saved_in, saved_pre, weights, norm_gain, norm_bias):
    f32, bf16 = jnp.float32, jnp.bfloat16
    half = lax.axis_index(HALF)
    core = lax.axis_index(CORE)
    layer = lax.axis_index(LAYER_AXIS)
    is_even = half == 0
    gain = lax.dynamic_index_in_dim(norm_gain, layer, 0, keepdims=False)
    offset_bias = lax.dynamic_index_in_dim(norm_bias, layer, 0, keepdims=False)
    weight = weights[0]
    stream, gradient = act_in[0], grad_in[0]
    features = weight.shape[0]
    hidden = weight.shape[1]
    tokens = hid_in.shape[1]
    cols = lax.axis_size(COLS)
    planes = lax.axis_size(PLANE)
    own = stream.shape[0]
    half_tokens = tokens // 2

    stream_float = stream.astype(f32)
    saved_float = saved_in[0].astype(f32)
    sums = lax.psum(
        jnp.stack(
            (
                jnp.sum(stream_float, axis=-1),
                jnp.sum(stream_float * stream_float, axis=-1),
                jnp.sum(saved_float, axis=-1),
                jnp.sum(saved_float * saved_float, axis=-1),
            )
        ),
        COLS,
    )
    stream_mean, stream_scale = statistics(sums[0], sums[1])
    saved_mean, saved_scale = statistics(sums[2], sums[3])
    normed = ((stream_float - stream_mean) * stream_scale * gain + offset_bias).astype(bf16)
    leading = jnp.where(is_even, normed, gradient)

    slope = gelu_slope(saved_pre[0].astype(f32), hid_in[0].astype(f32)).astype(bf16)
    right_side = jnp.where(is_even, slope, hid_in[0])
    right_side = right_side.reshape(planes, 2, own, hidden).transpose(1, 0, 2, 3)
    right_side = right_side.reshape(2, half_tokens, hidden)

    def product(which):
        rows = lax.dynamic_index_in_dim(right_side, which, 0, keepdims=False)
        return lax.dot_general(rows, weight, (((1,), (1,)), ((), ())), preferred_element_type=f32)

    swap = [(0, 1), (1, 0)]
    arriving = lax.ppermute(product(1 - core).astype(bf16), CORE, swap)
    chip_sum = (product(core) + arriving.astype(f32)).astype(bf16)

    outgoing = jnp.concatenate(
        (
            chip_sum.reshape(planes, own, features),
            jnp.broadcast_to(leading[None], (planes, own, features)),
        ),
        axis=1,
    )
    incoming = lax.all_to_all(outgoing, PLANE, 0, 0, tiled=True)
    term = jnp.sum(incoming[:, :own].astype(f32), axis=0)
    near = incoming[:, own:].reshape(half_tokens, features)
    far = lax.ppermute(near, CORE, swap)

    forward_odd = (stream_float + term).astype(bf16)
    act_next = boundary(jnp.where(is_even, stream, forward_odd), 1)
    saved_hat = (saved_float - saved_mean) * saved_scale
    scaled = term * gain
    moments = jnp.stack((jnp.sum(scaled, axis=-1), jnp.sum(scaled * saved_hat, axis=-1)))

    near_product = jnp.dot(near, weight, preferred_element_type=f32)
    far_product = jnp.dot(far, weight, preferred_element_type=f32)
    first = core == 0
    partial = jnp.stack(
        (jnp.where(first, near_product, far_product), jnp.where(first, far_product, near_product))
    )
    part = hidden // cols
    partial = partial.reshape(tokens, cols, part).transpose(1, 0, 2)
    extra = jnp.pad(moments.reshape(1, -1), ((0, 7), (0, part - moments.size)))
    partial = jnp.concatenate((partial, jnp.broadcast_to(extra[None], (cols, 8, part))), axis=1)
    summed = jnp.sum(lax.all_to_all(partial, COLS, 0, 0, tiled=True), axis=0)
    moments = summed[tokens, : moments.size].reshape(moments.shape)
    summed = summed[:tokens]
    hidden_value = jnp.where(is_even, jax.nn.gelu(summed, approximate=True), summed).astype(bf16)

    outgoing = jnp.broadcast_to(hidden_value[None], (2 * cols, tokens, part))
    incoming = lax.all_to_all(outgoing, (HALF, COLS), 0, 0, tiled=True)
    incoming = lax.dynamic_index_in_dim(
        incoming.reshape(2, cols, 2, planes, own, part), 1 - half, 0, keepdims=False
    )
    hidden_next = incoming.transpose(2, 1, 3, 0, 4).reshape(tokens, hidden)

    first_mean = (moments[0] / D)[:, None]
    second_mean = (moments[1] / D)[:, None]
    backward_even = (
        gradient.astype(f32) + saved_scale * (scaled - first_mean - saved_hat * second_mean)
    ).astype(bf16)
    grad_next = boundary(jnp.where(is_even, backward_even, gradient), -1)
    return (act_next[None], hidden_next[None], grad_next[None])


def solution(mesh):
    names = SECTION + ROWS + (COLS,)
    parts = Mesh(mesh.devices.reshape(2, 2, 4, 8, 2, 3), names)
    in_specs = (
        P(SECTION, ROWS, COLS),
        P(SECTION, None, ROWS),
        P(SECTION, ROWS, COLS),
        P(SECTION, ROWS, COLS),
        P(SECTION, None, ROWS),
        P(SECTION, COLS, ROWS),
        P(None, COLS),
        P(None, COLS),
    )
    out_specs = (P(SECTION, ROWS, COLS), P(SECTION, None, ROWS), P(SECTION, ROWS, COLS))
    return jax.shard_map(
        per_device, mesh=parts, in_specs=in_specs, out_specs=out_specs, check_vma=False
    )
```

```python
import jax
import jax.numpy as jnp
from jax import lax
from jax.experimental import pallas as pl
from jax.experimental.pallas import tpu as pltpu
from jax.sharding import Mesh, PartitionSpec as P

D = 12288
epsilon = 1e-05

LAYER_AXIS, HALF, COLS = "layer", "half", "cols"
PX, PY = "px", "py"
CORE = "core"
ROWS = (PX, PY, CORE)
SECTION = (LAYER_AXIS, HALF)


def statistics(total, squares):
    average = total / D
    inverse_scale = lax.rsqrt(squares / D - average * average + epsilon)
    return (average[:, None], inverse_scale[:, None])


def gelu_slope(preact, upstream):
    return jax.vjp(lambda value: jax.nn.gelu(value, approximate=True), preact)[1](upstream)[0]


def exchange(blocks, axis):
    return lax.all_to_all(blocks, axis, 0, 0, tiled=True)


def spread(block, axis):
    return exchange(jnp.broadcast_to(block[None], (lax.axis_size(axis), *block.shape)), axis)


def picked(rows, index):
    one_hot = (index[:, None] == jnp.arange(rows.shape[0])[None, :]).astype(rows.dtype)
    return jnp.dot(one_hot, rows, preferred_element_type=jnp.float32).astype(rows.dtype)


def high_low(values):
    high = values.astype(jnp.bfloat16)
    return high, (values - high.astype(jnp.float32)).astype(jnp.bfloat16)


def lane_groups(values):
    return sum(values[:, i : i + 128] for i in range(0, values.shape[1], 128))


def rows_step(rows_ref, vectors_ref, weight_ref, product, first, second):
    count = rows_ref.shape[0]
    floats = rows_ref[...].astype(jnp.float32)
    vectors = vectors_ref[...]
    pieces = high_low(floats * vectors[:1]) + high_low(vectors)
    left = jnp.concatenate(pieces, axis=0)
    result = jnp.dot(left, weight_ref[...], preferred_element_type=jnp.float32)
    more = result[2 * count :]
    product[:count] += result[:count] + result[count : 2 * count]
    product[count:] += more[:8] + more[8:]
    first[...] += lane_groups(floats)
    second[...] += lane_groups(floats * floats)


def near_kernel(rows_ref, vectors_ref, weight_ref, product, first, second):
    @pl.when(pl.program_id(0) == 0)
    def _():
        product[...] = jnp.zeros_like(product)
        first[...] = jnp.zeros_like(first)
        second[...] = jnp.zeros_like(second)

    rows_step(rows_ref, vectors_ref, weight_ref, product, first, second)


def far_kernel(
    rows_ref, vectors_ref, weight_ref, near_ref, near_first, near_second, payload, product, first, second
):
    near_kernel(rows_ref, vectors_ref, weight_ref, product, first, second)

    @pl.when(pl.program_id(0) == pl.num_programs(0) - 1)
    def _():
        count = rows_ref.shape[0]
        totals = [
            jnp.sum(jnp.concatenate((near[...], far[...]), axis=0).T, axis=0, keepdims=True)
            for near, far in ((near_first, first), (near_second, second))
        ]
        totals.append(jnp.zeros((4, 128), jnp.float32))
        for i in range(payload.shape[0]):
            part = slice(i * 128, (i + 1) * 128)
            payload[i, :count] = near_ref[:count, part]
            payload[i, count : 2 * count] = product[:count, part]
            payload[i, 2 * count :] = jnp.concatenate(
                [near_ref[count : count + 2, part]] + totals, axis=0
            )


STEPS = 4


def rows_call(kernel, rows, vectors, weight, near=None):
    count, features = rows.shape
    hidden = weight.shape[1]
    step = features // STEPS
    f32 = jnp.float32
    shapes = [(count + 8, hidden), (count, 128), (count, 128)]
    whole = [pl.BlockSpec(shape, lambda k: (0, 0)) for shape in shapes]
    specs = [
        pl.BlockSpec((count, step), lambda k: (0, k)),
        pl.BlockSpec((8, step), lambda k: (0, k)),
        pl.BlockSpec((step, hidden), lambda k: (k, 0)),
    ]
    if near is None:
        out_shape = [jax.ShapeDtypeStruct(shape, f32) for shape in shapes]
        out_specs, scratch, near = whole, [], ()
    else:
        out = (hidden // 128, 2 * count + 8, 128)
        out_shape = jax.ShapeDtypeStruct(out, f32)
        out_specs = pl.BlockSpec(out, lambda k: (0, 0, 0))
        specs = specs + whole
        scratch = [pltpu.VMEM(shape, f32) for shape in shapes]
    return pl.pallas_call(
        kernel,
        grid=(STEPS,),
        in_specs=specs,
        out_specs=out_specs,
        out_shape=out_shape,
        scratch_shapes=scratch,
        compiler_params=pltpu.CompilerParams(vmem_limit_bytes=24 * 2**20),
        cost_estimate=pl.CostEstimate(
            flops=4 * count * features * hidden, bytes_accessed=4 * 2**20, transcendentals=0
        ),
    )(rows, vectors, weight, *near)


def per_device(act_in, hid_in, grad_in, saved_in, saved_pre, weights, norm_gain, norm_bias):
    f32, bf16 = jnp.float32, jnp.bfloat16
    half = lax.axis_index(HALF)
    core = lax.axis_index(CORE)
    layer = lax.axis_index(LAYER_AXIS)
    is_even = half == 0
    gain = lax.dynamic_index_in_dim(norm_gain, layer, 0, keepdims=False)
    offset_bias = lax.dynamic_index_in_dim(norm_bias, layer, 0, keepdims=False)
    weight = weights[0]
    stream, gradient = act_in[0], grad_in[0]
    features, hidden = weight.shape
    tokens = hid_in.shape[1]
    own = stream.shape[0]
    nx, ny, cols = lax.axis_size(PX), lax.axis_size(PY), lax.axis_size(COLS)
    half_tokens = tokens // 2
    part = hidden // cols

    early = lax.ppermute(
        jnp.where(is_even, stream, gradient), SECTION, [(0, 1), (1, 0), (2, 3), (3, 2)]
    )

    token = jnp.arange(tokens)
    y_of, t_of = (token // own) % ny, token % own
    c_of, x_of = (token // (own * ny)) % 2, token // (own * ny * 2)
    slope = gelu_slope(saved_pre[0].astype(f32), hid_in[0].astype(f32)).astype(bf16)
    right_side = jnp.where(is_even, slope, hid_in[0])
    right_side = picked(right_side, ((x_of * ny + y_of) * 2 + c_of) * own + t_of)
    row_terms = lax.dot_general(
        right_side, weight, (((1,), (1,)), ((), ())), preferred_element_type=f32
    ).astype(bf16)
    chip_blocks = exchange(row_terms.reshape(nx * 2, ny * own, features), (PX, CORE))
    chip_sum = jnp.sum(chip_blocks.astype(f32), axis=0).astype(bf16)
    y_blocks = exchange(chip_sum.reshape(ny, own, features), PY)
    term = jnp.sum(y_blocks.astype(f32), axis=0)

    leading = jnp.where(is_even, stream, gradient)
    near = spread(leading, PY).reshape(ny * own, features)
    near = jnp.concatenate(
        [near]
        + [lax.ppermute(near, PX, [(i, (i + k) % nx) for i in range(nx)]) for k in range(1, nx)]
    )
    far = lax.ppermute(near, CORE, [(0, 1), (1, 0)])
    factor = jnp.where(is_even, gain, 1.0)
    vectors = jnp.concatenate(
        (factor[None], offset_bias[None], jnp.zeros((6, features), f32))
    )
    near_parts = rows_call(near_kernel, near, vectors, weight)
    payload = rows_call(far_kernel, far, vectors, weight, near_parts)

    stream_float = stream.astype(f32)
    saved_float = saved_in[0].astype(f32)
    scaled = term * gain
    moments = jnp.stack(
        (
            jnp.sum(saved_float, axis=-1),
            jnp.sum(saved_float * saved_float, axis=-1),
            jnp.sum(scaled, axis=-1),
            jnp.sum(scaled * saved_float, axis=-1),
        )
    ).reshape(1, -1)

    moments = jnp.pad(moments, ((0, 0), (0, 128 - moments.size)))
    payload = payload.at[:, tokens + 4].set(moments)
    summed = jnp.sum(exchange(payload, COLS), axis=0)
    totals = summed[tokens + 2 : tokens + 4]
    mean, scale = statistics(totals[0], totals[1])
    preact = scale * (summed[:tokens] - mean * summed[tokens]) + summed[tokens + 1]
    hidden_value = jnp.where(
        is_even, jax.nn.gelu(preact, approximate=True), summed[:tokens]
    ).astype(bf16)
    other = ((token // own) % 2 != core).astype(jnp.int32)
    behind = (lax.axis_index(PX) - token // (2 * own * ny)) % nx
    place = ((other * nx + behind) * ny + (token // (2 * own)) % ny) * own + t_of
    hidden_value = picked(hidden_value, place)

    incoming = spread(hidden_value, (HALF, COLS)).reshape(2, cols, tokens, part)
    incoming = lax.dynamic_index_in_dim(incoming, 1 - half, 0, keepdims=False)
    hidden_next = jnp.concatenate([incoming[i] for i in range(cols)], axis=1)

    forward_odd = stream_float + term
    moments = summed[tokens + 4, : 4 * own].reshape(4, own)
    saved_mean, saved_scale = statistics(moments[0], moments[1])
    saved_hat = (saved_float - saved_mean) * saved_scale
    first_mean = moments[2][:, None] / D
    second_mean = saved_scale * (moments[3][:, None] / D - saved_mean * first_mean)
    backward_even = gradient.astype(f32) + saved_scale * (
        scaled - first_mean - saved_hat * second_mean
    )
    late = jnp.where(is_even, backward_even, forward_odd).astype(bf16)
    late = lax.ppermute(late, SECTION, [(0, 3), (3, 0), (1, 2), (2, 1)])

    act_next = jnp.where(is_even, late, early)
    grad_next = jnp.where(is_even, early, late)
    return (act_next[None], hidden_next[None], grad_next[None])


def solution(mesh):
    names = SECTION + ROWS + (COLS,)
    parts = Mesh(mesh.devices.reshape(2, 2, 4, 8, 2, 3), names)
    in_specs = (
        P(SECTION, ROWS, COLS),
        P(SECTION, None, ROWS),
        P(SECTION, ROWS, COLS),
        P(SECTION, ROWS, COLS),
        P(SECTION, None, ROWS),
        P(SECTION, COLS, ROWS),
        P(None, COLS),
        P(None, COLS),
    )
    out_specs = (P(SECTION, ROWS, COLS), P(SECTION, None, ROWS), P(SECTION, ROWS, COLS))
    return jax.shard_map(
        per_device, mesh=parts, in_specs=in_specs, out_specs=out_specs, check_vma=False
    )
```

```python
import jax
import jax.numpy as jnp
from jax import lax
from jax.experimental import pallas as pl
from jax.experimental.pallas import tpu as pltpu
from jax.sharding import Mesh, PartitionSpec as P

D = 12288
epsilon = 1e-05

LAYER_AXIS, HALF, COLS = "layer", "half", "cols"
PX, PY = "px", "py"
CORE = "core"
ROWS = (PX, PY, CORE)
SECTION = (LAYER_AXIS, HALF)


def gelu_slope(preact, upstream):
    return jax.vjp(lambda value: jax.nn.gelu(value, approximate=True), preact)[1](upstream)[0]


def exchange(blocks, axis):
    return lax.all_to_all(blocks, axis, 0, 0, tiled=True)


def copies(block, axis):
    return jnp.broadcast_to(block[None], (lax.axis_size(axis), *block.shape))


def picked(rows, index):
    one_hot = (index[:, None] == jnp.arange(rows.shape[0])[None, :]).astype(rows.dtype)
    return jnp.dot(one_hot, rows, preferred_element_type=jnp.float32).astype(rows.dtype)


def high_low(values):
    high = values.astype(jnp.bfloat16)
    return high, (values - high.astype(jnp.float32)).astype(jnp.bfloat16)


def lane_groups(values):
    return sum(values[:, i : i + 128] for i in range(0, values.shape[1], 128))


def rows_step(rows, vectors_ref, weight_ref, result_ref):
    count = rows.shape[0]

    @pl.when(pl.program_id(0) == 0)
    def _():
        result_ref[...] = jnp.zeros_like(result_ref)

    floats = rows.astype(jnp.float32)
    vectors = vectors_ref[...]
    pieces = high_low(floats * vectors[:1]) + high_low(vectors)
    left = jnp.concatenate(pieces, axis=0)
    result = jnp.dot(left, weight_ref[...], preferred_element_type=jnp.float32)
    more = result[2 * count :]
    result_ref[:count] += result[:count] + result[count : 2 * count]
    result_ref[count : count + 8] += more[:8] + more[8:]
    result_ref[count + 8 :, :128] += lane_groups(floats)
    result_ref[count + 8 :, 128:256] += lane_groups(floats * floats)


def near_kernel(rows_ref, vectors_ref, weight_ref, result_ref):
    rows_step(rows_ref[...], vectors_ref, weight_ref, result_ref)


def far_kernel(rows_ref, vectors_ref, weight_ref, near_ref, payload, result_ref):
    rows_step(rows_ref[...], vectors_ref, weight_ref, result_ref)

    @pl.when(pl.program_id(0) == pl.num_programs(0) - 1)
    def _():
        count = rows_ref.shape[0]
        both = jnp.concatenate((near_ref[count + 8 :, :256], result_ref[count + 8 :, :256]), axis=0)
        totals = [
            jnp.sum(both[:, i : i + 128].T, axis=0, keepdims=True) for i in (0, 128)
        ] + [jnp.zeros((4, 128), jnp.float32)]
        for i in range(payload.shape[0]):
            part = slice(i * 128, (i + 1) * 128)
            payload[i, :count] = near_ref[:count, part]
            payload[i, count : 2 * count] = result_ref[:count, part]
            payload[i, 2 * count :] = jnp.concatenate(
                [near_ref[count : count + 2, part]] + totals, axis=0
            )


STEPS = 4
VMEM_LIMIT = 16 * 2**20


def rows_call(kernel, blocks, vectors, weight, near=None):
    count = sum(block.shape[0] for block in blocks)
    features, hidden = weight.shape
    step = features // STEPS
    f32 = jnp.float32
    shape = (2 * count + 8, hidden)
    whole = pl.BlockSpec(shape, lambda k: (0, 0))
    specs = [pl.BlockSpec((block.shape[0], step), lambda k: (0, k)) for block in blocks] + [
        pl.BlockSpec((8, step), lambda k: (0, k)),
        pl.BlockSpec((step, hidden), lambda k: (k, 0)),
    ]
    if near is None:
        out_shape, out_specs = jax.ShapeDtypeStruct(shape, f32), whole
        scratch, near = [], ()
    else:
        out = (hidden // 128, 2 * count + 8, 128)
        out_shape = jax.ShapeDtypeStruct(out, f32)
        out_specs = pl.BlockSpec(out, lambda k: (0, 0, 0))
        specs = specs + [whole]
        scratch, near = [pltpu.VMEM(shape, f32)], (near,)
    return pl.pallas_call(
        kernel,
        grid=(STEPS,),
        in_specs=specs,
        out_specs=out_specs,
        out_shape=out_shape,
        scratch_shapes=scratch,
        compiler_params=pltpu.CompilerParams(vmem_limit_bytes=VMEM_LIMIT),
        cost_estimate=pl.CostEstimate(flops=0, bytes_accessed=0, transcendentals=0),
    )(*blocks, vectors, weight, *near)


def blocks_of(values):
    row = lax.broadcasted_iota(jnp.int32, (8, 128), 0) // 2
    blocks = []
    for low in range(0, values.shape[0], 8):
        tiles = [values[low : low + 8, m * 128 : m * 128 + 128] for m in range(8)]
        for i in range(4):
            halves = []
            for first in (0, 4):
                half = jnp.zeros((8, 128), jnp.float32)
                for m in range(4):
                    moved = pltpu.roll(tiles[first + m], (2 * (m - i)) % 8, 0)
                    half = jnp.where(row == m, moved, half)
                halves.append(half)
            blocks.append(jnp.concatenate(halves, axis=0))
    return blocks


def terms_kernel(rows_ref, weight_ref, *refs):
    values = lax.dot_general(
        rows_ref[...],
        weight_ref[...],
        (((1,), (1,)), ((), ())),
        preferred_element_type=jnp.float32,
    )
    for p, block in enumerate(blocks_of(values)):
        if len(refs) == 2:
            block = block + refs[0][p].astype(jnp.float32)
        refs[-1][p] = block.astype(jnp.bfloat16)


def terms_call(rows, weight, *arriving):
    count, hidden = rows.shape
    features = weight.shape[0]
    block = pl.BlockSpec((count // 2, 16, 128), lambda k: (0, 0, k))
    return pl.pallas_call(
        terms_kernel,
        grid=(features // 1024,),
        in_specs=[
            pl.BlockSpec((count, hidden), lambda k: (0, 0)),
            pl.BlockSpec((1024, hidden), lambda k: (k, 0)),
        ]
        + [block] * len(arriving),
        out_specs=block,
        out_shape=jax.ShapeDtypeStruct((count // 2, 16, features // 8), jnp.bfloat16),
        compiler_params=pltpu.CompilerParams(vmem_limit_bytes=VMEM_LIMIT),
        cost_estimate=pl.CostEstimate(
            flops=2 * count * features * hidden, bytes_accessed=4 * 2**20, transcendentals=0
        ),
    )(rows, weight, *arriving)


def lines_of(values):
    values = values.reshape(-1, 2, 4, 8, 128).transpose(0, 3, 1, 2, 4)
    return values.reshape(-1, 16, 512)


def total(values):
    return jnp.sum(jnp.sum(values, axis=0, keepdims=True), axis=1, keepdims=True)


def finish_kernel(blocks, lines_ref, gain_ref, payload_in, term_ref, payload_out):
    term = jnp.sum(blocks[...].astype(jnp.float32), axis=0)
    term_ref[...] = term
    saved = lines_ref[0].astype(jnp.float32)
    scaled = term * gain_ref[...]
    lane = lax.broadcasted_iota(jnp.int32, (1, 128), 1)
    token_of = lax.broadcasted_iota(jnp.int32, saved.shape, 0) % 2
    moments = jnp.zeros((1, 128), jnp.float32)
    for i, values in enumerate((saved, saved * saved, scaled, scaled * saved)):
        for token in range(2):
            part = total(jnp.where(token_of == token, values, 0.0))
            moments = jnp.where(lane == 2 * i + token, part, moments)
    row = lax.broadcasted_iota(jnp.int32, (8, 128), 0)
    for i in range(payload_out.shape[0]):
        payload_out[i] = jnp.where(row == 4, moments, payload_in[i])


def finish_call(blocks, lines, gain, payload):
    vmem = pl.BlockSpec(memory_space=pltpu.VMEM)
    tail = pl.BlockSpec((payload.shape[0], 8, 128), lambda i: (0, payload.shape[1] // 8 - 1, 0))
    return pl.pallas_call(
        finish_kernel,
        grid=(1,),
        in_specs=[vmem, vmem, vmem, tail],
        out_specs=[vmem, tail],
        out_shape=[
            jax.ShapeDtypeStruct(gain.shape, jnp.float32),
            jax.ShapeDtypeStruct(payload.shape, payload.dtype),
        ],
        input_output_aliases={3: 1},
        compiler_params=pltpu.CompilerParams(vmem_limit_bytes=VMEM_LIMIT),
        cost_estimate=pl.CostEstimate(flops=2**20, bytes_accessed=2**20, transcendentals=0),
    )(blocks, lines, gain, payload)


def hidden_kernel(even_ref, received, order_ref, hidden_ref, moments_ref):
    f32, bf16 = jnp.float32, jnp.bfloat16
    tokens = order_ref.shape[0]
    summed = jnp.sum(received[...], axis=0)
    extra = summed[tokens:]
    moments_ref[...] = extra
    mean = extra[2:3] / D
    scale = lax.rsqrt(extra[3:4] / D - mean * mean + epsilon)
    columns = jnp.concatenate((scale, mean, jnp.zeros((tokens - 2, tokens), f32)), axis=0).T
    product = summed[:tokens]
    preact = columns[:, :1] * (product - columns[:, 1:2] * extra[:1]) + extra[1:2]
    gelu = jax.nn.gelu(preact, approximate=True)
    hidden = jnp.where(even_ref[0] == 1, gelu, product).astype(bf16)
    hidden = jnp.dot(order_ref[...], hidden, preferred_element_type=f32).astype(bf16)
    for i in range(hidden_ref.shape[0]):
        hidden_ref[i] = hidden


def late_kernel(even_ref, moments_ref, term_ref, lines_ref, gain_ref, late_ref):
    f32 = jnp.float32
    term = term_ref[...]
    saved, stream, gradient = (lines_ref[i].astype(f32) for i in range(3))
    token_of = lax.broadcasted_iota(jnp.int32, saved.shape, 0) % 2
    saved_total, saved_squares, scaled_total, scaled_saved = (
        jnp.where(token_of == 0, moments_ref[4:5, i : i + 1], moments_ref[4:5, i + 1 : i + 2])
        for i in range(0, 8, 2)
    )
    saved_mean = saved_total / D
    saved_scale = lax.rsqrt(saved_squares / D - saved_mean * saved_mean + epsilon)
    first_mean = scaled_total / D
    second_mean = saved_scale * (scaled_saved / D - saved_mean * first_mean)
    saved_hat = (saved - saved_mean) * saved_scale
    change = saved_scale * (term * gain_ref[...] - first_mean - saved_hat * second_mean)
    late = jnp.where(even_ref[0] == 1, gradient + change, stream + term)
    late_ref[...] = late.astype(jnp.bfloat16)


def vmem_call(kernel, flag, out_shape, cost, *operands):
    vmem = pl.BlockSpec(memory_space=pltpu.VMEM)
    return pl.pallas_call(
        kernel,
        in_specs=[pl.BlockSpec(memory_space=pltpu.SMEM)] + [vmem] * len(operands),
        out_specs=[vmem] * len(out_shape),
        out_shape=out_shape,
        compiler_params=pltpu.CompilerParams(vmem_limit_bytes=VMEM_LIMIT),
        cost_estimate=pl.CostEstimate(flops=cost, bytes_accessed=cost, transcendentals=0),
    )(flag, *operands)


def per_device(act_in, hid_in, grad_in, saved_in, saved_pre, weights, norm_gain, norm_bias):
    f32, bf16 = jnp.float32, jnp.bfloat16
    half = lax.axis_index(HALF)
    core = lax.axis_index(CORE)
    layer = lax.axis_index(LAYER_AXIS)
    is_even = half == 0
    gain = lax.dynamic_index_in_dim(norm_gain, layer, 0, keepdims=False)
    offset_bias = lax.dynamic_index_in_dim(norm_bias, layer, 0, keepdims=False)
    weight = weights[0]
    stream, gradient = act_in[0], grad_in[0]
    features, hidden = weight.shape
    tokens = hid_in.shape[1]
    own = stream.shape[0]
    nx, ny, cols = lax.axis_size(PX), lax.axis_size(PY), lax.axis_size(COLS)
    half_tokens = tokens // 2
    part = hidden // cols

    early = lax.ppermute(
        jnp.where(is_even, stream, gradient), SECTION, [(0, 1), (1, 0), (2, 3), (3, 2)]
    )

    leading = copies(jnp.where(is_even, stream, gradient), PY)

    token = jnp.arange(tokens)
    t_of = token % own
    slope = gelu_slope(saved_pre[0].astype(f32), hid_in[0].astype(f32)).astype(bf16)
    right_side = jnp.where(is_even, slope, hid_in[0])
    row, group = token % half_tokens, token // half_tokens
    right_side = picked(right_side, (row // own * 2 + (group != core)) * own + row % own)
    own_x = exchange(leading, PY).reshape(ny * own, features)
    cores = [(0, 1), (1, 0)]
    arriving = lax.ppermute(terms_call(right_side[half_tokens:], weight), CORE, cores)
    own_x, own_rows = lax.optimization_barrier((own_x, right_side[:half_tokens]))
    chip_terms = terms_call(own_rows, weight, arriving)
    own_x, chip_terms = lax.optimization_barrier((own_x, chip_terms))
    term_blocks = exchange(chip_terms, (PX, PY))

    near = lax.all_gather(own_x, PX, axis=0, tiled=True)
    far = lax.ppermute(near, CORE, cores)
    factor = jnp.where(is_even, gain, 1.0)
    vectors = jnp.concatenate(
        (factor[None], offset_bias[None], jnp.zeros((6, features), f32))
    )
    near_parts = rows_call(near_kernel, [near], vectors, weight)
    payload = rows_call(far_kernel, [far], vectors, weight, near_parts)

    line_gain = lines_of(jnp.broadcast_to(gain[None], (own, features)))[0]
    lines = lines_of(jnp.stack((saved_in[0], stream, gradient)))
    term, payload = finish_call(term_blocks, lines, line_gain, payload)
    other = ((token // own) % 2 != core).astype(jnp.int32)
    x_of = token // (2 * own * ny)
    place = ((other * nx + x_of) * ny + (token // (2 * own)) % ny) * own + t_of
    order = (place[:, None] == token[None, :]).astype(bf16)
    received, early = lax.optimization_barrier((exchange(payload, COLS), early))
    flag = is_even.astype(jnp.int32).reshape(1)
    hidden_value, moments = vmem_call(
        hidden_kernel,
        flag,
        [
            jax.ShapeDtypeStruct((2 * cols, tokens, part), bf16),
            jax.ShapeDtypeStruct((8, part), f32),
        ],
        0,
        received,
        order,
    )
    (late,) = vmem_call(
        late_kernel,
        flag,
        [jax.ShapeDtypeStruct(term.shape, bf16)],
        2**24,
        moments,
        term,
        lines,
        line_gain,
    )

    incoming = exchange(hidden_value, (HALF, COLS)).reshape(2, cols, tokens, part)
    incoming = lax.dynamic_index_in_dim(incoming, 1 - half, 0, keepdims=False)
    hidden_next = jnp.concatenate([incoming[i] for i in range(cols)], axis=1)

    late = lax.ppermute(late, SECTION, [(0, 3), (3, 0), (1, 2), (2, 1)])
    late = late.reshape(8, own, 4, 128).transpose(1, 2, 0, 3).reshape(own, features)

    act_next = jnp.where(is_even, late, early)
    grad_next = jnp.where(is_even, early, late)
    return (act_next[None], hidden_next[None], grad_next[None])


def solution(mesh):
    names = SECTION + ROWS + (COLS,)
    parts = Mesh(mesh.devices.reshape(2, 2, 4, 8, 2, 3), names)
    in_specs = (
        P(SECTION, ROWS, COLS),
        P(SECTION, None, ROWS),
        P(SECTION, ROWS, COLS),
        P(SECTION, ROWS, COLS),
        P(SECTION, None, ROWS),
        P(SECTION, COLS, ROWS),
        P(None, COLS),
        P(None, COLS),
    )
    out_specs = (P(SECTION, ROWS, COLS), P(SECTION, None, ROWS), P(SECTION, ROWS, COLS))
    return jax.shard_map(
        per_device, mesh=parts, in_specs=in_specs, out_specs=out_specs, check_vma=False
    )
```

```python
import jax
import jax.numpy as jnp
from jax import lax
from jax.experimental import pallas as pl
from jax.experimental.pallas import tpu as pltpu
from jax.sharding import Mesh, PartitionSpec as P

D = 12288
epsilon = 1e-05

LAYER_AXIS, HALF, COLS = "layer", "half", "cols"
PX, PY = "px", "py"
CORE = "core"
PLANE = (PX, PY)
ROWS = PLANE + (CORE,)
SECTION = (LAYER_AXIS, HALF)


def gelu_slope(preact, upstream):
    return jax.vjp(lambda value: jax.nn.gelu(value, approximate=True), preact)[1](upstream)[0]


def exchange(blocks, axis):
    return lax.all_to_all(blocks, axis, 0, 0, tiled=True)


def copies(block, axis):
    return jnp.broadcast_to(block[None], (lax.axis_size(axis), *block.shape))


def picked(rows, index):
    one_hot = (index[:, None] == jnp.arange(rows.shape[0])[None, :]).astype(rows.dtype)
    return jnp.dot(one_hot, rows, preferred_element_type=jnp.float32).astype(rows.dtype)


def high_low(values):
    high = values.astype(jnp.bfloat16)
    return high, (values - high.astype(jnp.float32)).astype(jnp.bfloat16)


def lane_groups(values):
    return sum(values[:, i : i + 128] for i in range(0, values.shape[1], 128))


def rows_step(rows, vectors_ref, weight_ref, result_ref):
    count = rows.shape[0]

    @pl.when(pl.program_id(0) == 0)
    def _():
        result_ref[...] = jnp.zeros_like(result_ref)

    floats = rows.astype(jnp.float32)
    vectors = vectors_ref[...]
    pieces = high_low(floats * vectors[:1]) + high_low(vectors)
    left = jnp.concatenate(pieces, axis=0)
    result = jnp.dot(left, weight_ref[...], preferred_element_type=jnp.float32)
    more = result[2 * count :]
    result_ref[:count] += result[:count] + result[count : 2 * count]
    result_ref[count : count + 8] += more[:8] + more[8:]
    result_ref[count + 8 :, :128] += lane_groups(floats)
    result_ref[count + 8 :, 128:256] += lane_groups(floats * floats)


def near_kernel(rows_ref, vectors_ref, weight_ref, result_ref):
    rows_step(rows_ref[...], vectors_ref, weight_ref, result_ref)


def far_kernel(rows_ref, vectors_ref, weight_ref, near_ref, payload, result_ref):
    rows_step(rows_ref[...], vectors_ref, weight_ref, result_ref)

    @pl.when(pl.program_id(0) == pl.num_programs(0) - 1)
    def _():
        count = rows_ref.shape[0]
        both = jnp.concatenate((near_ref[count + 8 :, :256], result_ref[count + 8 :, :256]), axis=0)
        totals = [
            jnp.sum(both[:, i : i + 128].T, axis=0, keepdims=True) for i in (0, 128)
        ] + [jnp.zeros((4, 128), jnp.float32)]
        for i in range(payload.shape[0]):
            part = slice(i * 128, (i + 1) * 128)
            payload[i, :count] = near_ref[:count, part]
            payload[i, count : 2 * count] = result_ref[:count, part]
            payload[i, 2 * count :] = jnp.concatenate(
                [near_ref[count : count + 2, part]] + totals, axis=0
            )


STEPS = 4
VMEM_LIMIT = 16 * 2**20


def rows_call(kernel, blocks, vectors, weight, near=None):
    count = sum(block.shape[0] for block in blocks)
    features, hidden = weight.shape
    step = features // STEPS
    f32 = jnp.float32
    shape = (2 * count + 8, hidden)
    whole = pl.BlockSpec(shape, lambda k: (0, 0))
    specs = [pl.BlockSpec((block.shape[0], step), lambda k: (0, k)) for block in blocks] + [
        pl.BlockSpec((8, step), lambda k: (0, k)),
        pl.BlockSpec((step, hidden), lambda k: (k, 0)),
    ]
    if near is None:
        out_shape, out_specs = jax.ShapeDtypeStruct(shape, f32), whole
        scratch, near = [], ()
    else:
        out = (hidden // 128, 2 * count + 8, 128)
        out_shape = jax.ShapeDtypeStruct(out, f32)
        out_specs = pl.BlockSpec(out, lambda k: (0, 0, 0))
        specs = specs + [whole]
        scratch, near = [pltpu.VMEM(shape, f32)], (near,)
    return pl.pallas_call(
        kernel,
        grid=(STEPS,),
        in_specs=specs,
        out_specs=out_specs,
        out_shape=out_shape,
        scratch_shapes=scratch,
        compiler_params=pltpu.CompilerParams(vmem_limit_bytes=VMEM_LIMIT),
        cost_estimate=pl.CostEstimate(flops=0, bytes_accessed=0, transcendentals=0),
    )(*blocks, vectors, weight, *near)


def blocks_of(values):
    row = lax.broadcasted_iota(jnp.int32, (8, 128), 0) // 2
    blocks = []
    for low in range(0, values.shape[0], 8):
        tiles = [values[low : low + 8, m * 128 : m * 128 + 128] for m in range(8)]
        for i in range(4):
            halves = []
            for first in (0, 4):
                half = jnp.zeros((8, 128), jnp.float32)
                for m in range(4):
                    moved = pltpu.roll(tiles[first + m], (2 * (m - i)) % 8, 0)
                    half = jnp.where(row == m, moved, half)
                halves.append(half)
            blocks.append(jnp.concatenate(halves, axis=0))
    return blocks


def terms_kernel(rows_ref, weight_ref, own_ref, other_ref):
    values = lax.dot_general(
        rows_ref[...],
        weight_ref[...],
        (((1,), (1,)), ((), ())),
        preferred_element_type=jnp.float32,
    )
    half = values.shape[0] // 2
    for p, block in enumerate(blocks_of(values[half:])):
        other_ref[p] = block.astype(jnp.bfloat16)
    for p, block in enumerate(blocks_of(values[:half])):
        own_ref[p] = block


def terms_call(rows, weight):
    count, hidden = rows.shape
    features = weight.shape[0]
    block = pl.BlockSpec((count // 4, 16, 128), lambda k: (0, 0, k))
    shape = (count // 4, 16, features // 8)
    return pl.pallas_call(
        terms_kernel,
        grid=(features // 1024,),
        in_specs=[
            pl.BlockSpec((count, hidden), lambda k: (0, 0)),
            pl.BlockSpec((1024, hidden), lambda k: (k, 0)),
        ],
        out_specs=[block, block],
        out_shape=[
            jax.ShapeDtypeStruct(shape, jnp.float32),
            jax.ShapeDtypeStruct(shape, jnp.bfloat16),
        ],
        compiler_params=pltpu.CompilerParams(vmem_limit_bytes=VMEM_LIMIT),
        cost_estimate=pl.CostEstimate(flops=0, bytes_accessed=0, transcendentals=0),
    )(rows, weight)


def zero_kernel(anything_ref, zero_ref):
    zero_ref[...] = jnp.zeros_like(zero_ref)


def zero_after(anything):
    zeros = pl.pallas_call(
        zero_kernel,
        in_specs=[pl.BlockSpec(memory_space=pl.ANY)],
        out_specs=pl.BlockSpec(memory_space=pltpu.VMEM),
        out_shape=jax.ShapeDtypeStruct((8, 128), jnp.float32),
        compiler_params=pltpu.CompilerParams(vmem_limit_bytes=2**20),
        cost_estimate=pl.CostEstimate(flops=2**35, bytes_accessed=2**26, transcendentals=0),
    )(anything)
    return zeros[0, 0]


def lines_of(values):
    values = values.reshape(-1, 2, 4, 8, 128).transpose(0, 3, 1, 2, 4)
    return values.reshape(-1, 16, 512)


def total(values):
    return jnp.sum(jnp.sum(values, axis=0, keepdims=True), axis=1, keepdims=True)


def finish_kernel(blocks, lines_ref, gain_ref, payload_in, term_ref, payload_out):
    term = jnp.sum(blocks[...].astype(jnp.float32), axis=0)
    term_ref[...] = term
    saved = lines_ref[0].astype(jnp.float32)
    scaled = term * gain_ref[...]
    lane = lax.broadcasted_iota(jnp.int32, (1, 128), 1)
    token_of = lax.broadcasted_iota(jnp.int32, saved.shape, 0) % 2
    moments = jnp.zeros((1, 128), jnp.float32)
    for i, values in enumerate((saved, saved * saved, scaled, scaled * saved)):
        for token in range(2):
            part = total(jnp.where(token_of == token, values, 0.0))
            moments = jnp.where(lane == 2 * i + token, part, moments)
    row = lax.broadcasted_iota(jnp.int32, (8, 128), 0)
    for i in range(payload_out.shape[0]):
        payload_out[i] = jnp.where(row == 4, moments, payload_in[i])


def finish_call(blocks, lines, gain, payload):
    vmem = pl.BlockSpec(memory_space=pltpu.VMEM)
    tail = pl.BlockSpec((payload.shape[0], 8, 128), lambda i: (0, payload.shape[1] // 8 - 1, 0))
    return pl.pallas_call(
        finish_kernel,
        grid=(1,),
        in_specs=[vmem, vmem, vmem, tail],
        out_specs=[vmem, tail],
        out_shape=[
            jax.ShapeDtypeStruct(gain.shape, jnp.float32),
            jax.ShapeDtypeStruct(payload.shape, payload.dtype),
        ],
        input_output_aliases={3: 1},
        compiler_params=pltpu.CompilerParams(vmem_limit_bytes=VMEM_LIMIT),
        cost_estimate=pl.CostEstimate(flops=2**20, bytes_accessed=2**20, transcendentals=0),
    )(blocks, lines, gain, payload)


def hidden_kernel(even_ref, received, order_ref, hidden_ref, moments_ref):
    f32, bf16 = jnp.float32, jnp.bfloat16
    tokens = order_ref.shape[0]
    summed = jnp.sum(received[...], axis=0)
    extra = summed[tokens:]
    moments_ref[...] = extra
    mean = extra[2:3] / D
    scale = lax.rsqrt(extra[3:4] / D - mean * mean + epsilon)
    columns = jnp.concatenate((scale, mean, jnp.zeros((tokens - 2, tokens), f32)), axis=0).T
    product = summed[:tokens]
    preact = columns[:, :1] * (product - columns[:, 1:2] * extra[:1]) + extra[1:2]
    gelu = jax.nn.gelu(preact, approximate=True)
    hidden = jnp.where(even_ref[0] == 1, gelu, product).astype(bf16)
    hidden = jnp.dot(order_ref[...], hidden, preferred_element_type=f32).astype(bf16)
    for i in range(hidden_ref.shape[0]):
        hidden_ref[i] = hidden


def late_kernel(even_ref, moments_ref, term_ref, lines_ref, gain_ref, late_ref):
    f32 = jnp.float32
    term = term_ref[...]
    saved, stream, gradient = (lines_ref[i].astype(f32) for i in range(3))
    token_of = lax.broadcasted_iota(jnp.int32, saved.shape, 0) % 2
    saved_total, saved_squares, scaled_total, scaled_saved = (
        jnp.where(token_of == 0, moments_ref[4:5, i : i + 1], moments_ref[4:5, i + 1 : i + 2])
        for i in range(0, 8, 2)
    )
    saved_mean = saved_total / D
    saved_scale = lax.rsqrt(saved_squares / D - saved_mean * saved_mean + epsilon)
    first_mean = scaled_total / D
    second_mean = saved_scale * (scaled_saved / D - saved_mean * first_mean)
    saved_hat = (saved - saved_mean) * saved_scale
    change = saved_scale * (term * gain_ref[...] - first_mean - saved_hat * second_mean)
    late = jnp.where(even_ref[0] == 1, gradient + change, stream + term)
    late_ref[...] = late.astype(jnp.bfloat16)


def assemble_kernel(half_ref, *refs):
    blocks, hidden_ref = refs[:-1], refs[-1]
    cols = len(blocks)
    for i in range(cols):
        hidden_ref[:, i * 128 : i * 128 + 128] = blocks[i][0]


def assemble_call(half, incoming):
    cols, (tokens, part) = incoming.shape[0] // 2, incoming.shape[1:]

    def block(i):
        return pl.BlockSpec((1, tokens, part), lambda k, half: ((1 - half[0]) * cols + i, 0, 0))

    return pl.pallas_call(
        assemble_kernel,
        grid_spec=pltpu.PrefetchScalarGridSpec(
            num_scalar_prefetch=1,
            grid=(1,),
            in_specs=[block(i) for i in range(cols)],
            out_specs=pl.BlockSpec((tokens, cols * part), lambda k, half: (0, 0)),
        ),
        out_shape=jax.ShapeDtypeStruct((tokens, cols * part), incoming.dtype),
        compiler_params=pltpu.CompilerParams(vmem_limit_bytes=VMEM_LIMIT),
        cost_estimate=pl.CostEstimate(flops=2**35, bytes_accessed=2**26, transcendentals=0),
    )(half.astype(jnp.int32).reshape(1), *[incoming] * cols)


def vmem_call(kernel, flag, out_shape, cost, *operands):
    vmem = pl.BlockSpec(memory_space=pltpu.VMEM)
    return pl.pallas_call(
        kernel,
        in_specs=[pl.BlockSpec(memory_space=pltpu.SMEM)] + [vmem] * len(operands),
        out_specs=[vmem] * len(out_shape),
        out_shape=out_shape,
        compiler_params=pltpu.CompilerParams(vmem_limit_bytes=VMEM_LIMIT),
        cost_estimate=pl.CostEstimate(flops=cost, bytes_accessed=cost, transcendentals=0),
    )(flag, *operands)


def per_device(act_in, hid_in, grad_in, saved_in, saved_pre, weights, norm_gain, norm_bias):
    f32, bf16 = jnp.float32, jnp.bfloat16
    half = lax.axis_index(HALF)
    core = lax.axis_index(CORE)
    layer = lax.axis_index(LAYER_AXIS)
    is_even = half == 0
    gain = lax.dynamic_index_in_dim(norm_gain, layer, 0, keepdims=False)
    offset_bias = lax.dynamic_index_in_dim(norm_bias, layer, 0, keepdims=False)
    weight = weights[0]
    stream, gradient = act_in[0], grad_in[0]
    features, hidden = weight.shape
    tokens = hid_in.shape[1]
    own = stream.shape[0]
    nx, ny, cols = lax.axis_size(PX), lax.axis_size(PY), lax.axis_size(COLS)
    half_tokens = tokens // 2
    part = hidden // cols

    early = jnp.where(is_even, *lax.optimization_barrier((stream, gradient)))
    early = lax.ppermute(early, SECTION, [(0, 1), (1, 0), (2, 3), (3, 2)])

    leading = copies(jnp.where(is_even, stream, gradient), PLANE)

    token = jnp.arange(tokens)
    t_of = token % own
    slope = gelu_slope(saved_pre[0].astype(f32), hid_in[0].astype(f32)).astype(bf16)
    right_side = jnp.where(is_even, slope, hid_in[0])
    row, group = token % half_tokens, token // half_tokens
    right_side = picked(right_side, (row // own * 2 + (group != core)) * own + row % own)
    near = exchange(leading, PLANE)
    cores = [(0, 1), (1, 0)]
    own_terms, other_terms = terms_call(right_side, weight)
    arriving = lax.ppermute(other_terms, CORE, cores)
    chip_terms = (own_terms + (arriving.astype(f32) + zero_after(near))).astype(bf16)
    near, chip_terms = lax.optimization_barrier((near, chip_terms))
    term_blocks = exchange(chip_terms, PLANE)

    near = near.reshape(half_tokens, features)
    far = lax.ppermute(near, CORE, cores)
    factor = jnp.where(is_even, gain, 1.0)
    vectors = jnp.concatenate(
        (factor[None], offset_bias[None], jnp.zeros((6, features), f32))
    )
    near_parts = rows_call(near_kernel, [near], vectors, weight)
    payload = rows_call(far_kernel, [far], vectors, weight, near_parts)

    line_gain = lines_of(jnp.broadcast_to(gain[None], (own, features)))[0]
    lines = lines_of(jnp.stack((saved_in[0], stream, gradient)))
    term, payload = finish_call(term_blocks, lines, line_gain + zero_after(term_blocks), payload)
    other = ((token // own) % 2 != core).astype(jnp.int32)
    x_of = token // (2 * own * ny)
    place = ((other * nx + x_of) * ny + (token // (2 * own)) % ny) * own + t_of
    order = (place[:, None] == token[None, :]).astype(bf16)
    payload, early = lax.optimization_barrier((payload, early))
    received = exchange(payload, COLS)
    flag = is_even.astype(jnp.int32).reshape(1)
    hidden_value, moments = vmem_call(
        hidden_kernel,
        flag,
        [
            jax.ShapeDtypeStruct((2 * cols, tokens, part), bf16),
            jax.ShapeDtypeStruct((8, part), f32),
        ],
        0,
        received,
        order,
    )
    (late,) = vmem_call(
        late_kernel,
        flag,
        [jax.ShapeDtypeStruct(term.shape, bf16)],
        2**24,
        moments,
        term,
        lines,
        line_gain,
    )

    incoming = exchange(hidden_value, (HALF, COLS))
    hidden_next = assemble_call(half, incoming)

    late = lax.ppermute(late, SECTION, [(0, 3), (3, 0), (1, 2), (2, 1)])
    late = late.reshape(8, own, 4, 128).transpose(1, 2, 0, 3).reshape(own, features)

    late, hidden_next = lax.optimization_barrier((late, hidden_next))
    act_next = jnp.where(is_even, late, early)
    grad_next = jnp.where(is_even, early, late)
    return (act_next[None], hidden_next[None], grad_next[None])


def solution(mesh):
    names = SECTION + ROWS + (COLS,)
    parts = Mesh(mesh.devices.reshape(2, 2, 4, 8, 2, 3), names)
    in_specs = (
        P(SECTION, ROWS, COLS),
        P(SECTION, None, ROWS),
        P(SECTION, ROWS, COLS),
        P(SECTION, ROWS, COLS),
        P(SECTION, None, ROWS),
        P(SECTION, COLS, ROWS),
        P(None, COLS),
        P(None, COLS),
    )
    out_specs = (P(SECTION, ROWS, COLS), P(SECTION, None, ROWS), P(SECTION, ROWS, COLS))
    return jax.shard_map(
        per_device, mesh=parts, in_specs=in_specs, out_specs=out_specs, check_vma=False
    )
```

```python
import jax
import jax.numpy as jnp
from jax import lax
from jax.experimental import pallas as pl
from jax.experimental.pallas import tpu as pltpu
from jax.sharding import Mesh, PartitionSpec as P

D = 12288
epsilon = 1e-05

LAYER_AXIS, HALF, COLS = "layer", "half", "cols"
PX, PY = "px", "py"
CORE = "core"
PLANE = (PX, PY)
ROWS = PLANE + (CORE,)
SECTION = (LAYER_AXIS, HALF)


def gelu_slope(preact, upstream):
    return jax.vjp(lambda value: jax.nn.gelu(value, approximate=True), preact)[1](upstream)[0]


def exchange(blocks, axis):
    return lax.all_to_all(blocks, axis, 0, 0, tiled=True)


def copies(block, axis):
    return jnp.broadcast_to(block[None], (lax.axis_size(axis), *block.shape))


def picked(rows, index):
    one_hot = (index[:, None] == jnp.arange(rows.shape[0])[None, :]).astype(rows.dtype)
    return jnp.dot(one_hot, rows, preferred_element_type=jnp.float32).astype(rows.dtype)


def high_low(values):
    high = values.astype(jnp.bfloat16)
    return high, (values - high.astype(jnp.float32)).astype(jnp.bfloat16)


def lane_groups(values):
    return sum(values[:, i : i + 128] for i in range(0, values.shape[1], 128))


def rows_step(rows, vectors_ref, weight_ref, result_ref):
    count = rows.shape[0]

    @pl.when(pl.program_id(0) == 0)
    def _():
        result_ref[...] = jnp.zeros_like(result_ref)

    floats = rows.astype(jnp.float32)
    vectors = vectors_ref[...]
    pieces = high_low(floats * vectors[:1]) + high_low(vectors)
    left = jnp.concatenate(pieces, axis=0)
    result = jnp.dot(left, weight_ref[...], preferred_element_type=jnp.float32)
    more = result[2 * count :]
    result_ref[:count] += result[:count] + result[count : 2 * count]
    result_ref[count : count + 8] += more[:8] + more[8:]
    result_ref[count + 8 :, :128] += lane_groups(floats)
    result_ref[count + 8 :, 128:256] += lane_groups(floats * floats)


def near_kernel(rows_ref, vectors_ref, weight_ref, result_ref):
    rows_step(rows_ref[...], vectors_ref, weight_ref, result_ref)


def far_kernel(rows_ref, vectors_ref, weight_ref, near_ref, payload, result_ref):
    rows_step(rows_ref[...], vectors_ref, weight_ref, result_ref)

    @pl.when(pl.program_id(0) == pl.num_programs(0) - 1)
    def _():
        count = rows_ref.shape[0]
        both = jnp.concatenate((near_ref[count + 8 :, :256], result_ref[count + 8 :, :256]), axis=0)
        totals = [
            jnp.sum(both[:, i : i + 128].T, axis=0, keepdims=True) for i in (0, 128)
        ] + [jnp.zeros((4, 128), jnp.float32)]
        for i in range(payload.shape[0]):
            part = slice(i * 128, (i + 1) * 128)
            payload[i, :count] = near_ref[:count, part]
            payload[i, count : 2 * count] = result_ref[:count, part]
            payload[i, 2 * count :] = jnp.concatenate(
                [near_ref[count : count + 2, part]] + totals, axis=0
            )


STEPS = 4
VMEM_LIMIT = 12 * 2**20


def rows_call(kernel, blocks, vectors, weight, near=None):
    count = sum(block.shape[0] for block in blocks)
    features, hidden = weight.shape
    step = features // STEPS
    f32 = jnp.float32
    shape = (2 * count + 8, hidden)
    whole = pl.BlockSpec(shape, lambda k: (0, 0))
    specs = [pl.BlockSpec((block.shape[0], step), lambda k: (0, k)) for block in blocks] + [
        pl.BlockSpec((8, step), lambda k: (0, k)),
        pl.BlockSpec((step, hidden), lambda k: (k, 0)),
    ]
    if near is None:
        out_shape, out_specs = jax.ShapeDtypeStruct(shape, f32), whole
        scratch, near = [], ()
    else:
        out = (hidden // 128, 2 * count + 8, 128)
        out_shape = jax.ShapeDtypeStruct(out, f32)
        out_specs = pl.BlockSpec(out, lambda k: (0, 0, 0))
        specs = specs + [whole]
        scratch, near = [pltpu.VMEM(shape, f32)], (near,)
    return pl.pallas_call(
        kernel,
        grid=(STEPS,),
        in_specs=specs,
        out_specs=out_specs,
        out_shape=out_shape,
        scratch_shapes=scratch,
        compiler_params=pltpu.CompilerParams(vmem_limit_bytes=VMEM_LIMIT),
        cost_estimate=pl.CostEstimate(flops=0, bytes_accessed=0, transcendentals=0),
    )(*blocks, vectors, weight, *near)


def blocks_of(values):
    row = lax.broadcasted_iota(jnp.int32, (8, 128), 0) // 2
    blocks = []
    for low in range(0, values.shape[0], 8):
        tiles = [values[low : low + 8, m * 128 : m * 128 + 128] for m in range(8)]
        for i in range(4):
            halves = []
            for first in (0, 4):
                half = jnp.zeros((8, 128), jnp.float32)
                for m in range(4):
                    moved = pltpu.roll(tiles[first + m], (2 * (m - i)) % 8, 0)
                    half = jnp.where(row == m, moved, half)
                halves.append(half)
            blocks.append(jnp.concatenate(halves, axis=0))
    return blocks


def terms_kernel(rows_ref, weight_ref, own_ref, other_ref):
    values = lax.dot_general(
        rows_ref[...],
        weight_ref[...],
        (((1,), (1,)), ((), ())),
        preferred_element_type=jnp.float32,
    )
    half = values.shape[0] // 2
    for p, block in enumerate(blocks_of(values[half:])):
        other_ref[p] = block.astype(jnp.bfloat16)
    for p, block in enumerate(blocks_of(values[:half])):
        own_ref[p] = block


def terms_call(rows, weight):
    count, hidden = rows.shape
    features = weight.shape[0]
    block = pl.BlockSpec((count // 4, 16, 128), lambda k: (0, 0, k))
    shape = (count // 4, 16, features // 8)
    return pl.pallas_call(
        terms_kernel,
        grid=(features // 1024,),
        in_specs=[
            pl.BlockSpec((count, hidden), lambda k: (0, 0)),
            pl.BlockSpec((1024, hidden), lambda k: (k, 0)),
        ],
        out_specs=[block, block],
        out_shape=[
            pltpu.HBM(shape, jnp.float32),
            pltpu.HBM(shape, jnp.bfloat16),
        ],
        compiler_params=pltpu.CompilerParams(vmem_limit_bytes=VMEM_LIMIT),
        cost_estimate=pl.CostEstimate(flops=0, bytes_accessed=0, transcendentals=0),
    )(rows, weight)


def zero_kernel(anything_ref, zero_ref):
    zero_ref[...] = jnp.zeros_like(zero_ref)


def zero_after(anything):
    return pl.pallas_call(
        zero_kernel,
        in_specs=[pl.BlockSpec(memory_space=pl.ANY)],
        out_specs=pl.BlockSpec(memory_space=pltpu.VMEM),
        out_shape=jax.ShapeDtypeStruct((8, 128), jnp.float32),
        compiler_params=pltpu.CompilerParams(vmem_limit_bytes=2**20),
        cost_estimate=pl.CostEstimate(flops=2**35, bytes_accessed=2**26, transcendentals=0),
    )(pltpu.with_memory_space_constraint(anything, pltpu.HBM))


def add_kernel(own_ref, arriving_ref, zero_ref, sum_ref):
    values = own_ref[...] + arriving_ref[...].astype(jnp.float32)
    sum_ref[...] = (values + zero_ref[0, 0]).astype(jnp.bfloat16)


def add_call(own, arriving, zeros):
    block = pl.BlockSpec((own.shape[0] // 2, *own.shape[1:]), lambda k: (k, 0, 0))
    return pl.pallas_call(
        add_kernel,
        grid=(2,),
        in_specs=[block, block, pl.BlockSpec(zeros.shape, lambda k: (0, 0))],
        out_specs=block,
        out_shape=pltpu.HBM(own.shape, jnp.bfloat16),
        compiler_params=pltpu.CompilerParams(vmem_limit_bytes=VMEM_LIMIT),
        cost_estimate=pl.CostEstimate(flops=0, bytes_accessed=0, transcendentals=0),
    )(pltpu.with_memory_space_constraint(own, pltpu.HBM), arriving, zeros)


def lines_of(values):
    values = values.reshape(-1, 2, 4, 8, 128).transpose(0, 3, 1, 2, 4)
    return values.reshape(-1, 16, 512)


def total(values):
    return jnp.sum(jnp.sum(values, axis=0, keepdims=True), axis=1, keepdims=True)


def finish_kernel(blocks, lines_ref, gain_ref, zero_ref, payload_in, term_ref, payload_out):
    term = jnp.sum(blocks[...].astype(jnp.float32), axis=0) + zero_ref[0, 0]
    term_ref[...] = term
    saved = lines_ref[0].astype(jnp.float32)
    scaled = term * gain_ref[...]
    lane = lax.broadcasted_iota(jnp.int32, (1, 128), 1)
    token_of = lax.broadcasted_iota(jnp.int32, saved.shape, 0) % 2
    moments = jnp.zeros((1, 128), jnp.float32)
    for i, values in enumerate((saved, saved * saved, scaled, scaled * saved)):
        for token in range(2):
            part = total(jnp.where(token_of == token, values, 0.0))
            moments = jnp.where(lane == 2 * i + token, part, moments)
    row = lax.broadcasted_iota(jnp.int32, (8, 128), 0)
    for i in range(payload_out.shape[0]):
        payload_out[i] = jnp.where(row == 4, moments, payload_in[i])


def finish_call(blocks, lines, gain, zeros, payload):
    vmem = pl.BlockSpec(memory_space=pltpu.VMEM)
    tail = pl.BlockSpec((payload.shape[0], 8, 128), lambda i: (0, payload.shape[1] // 8 - 1, 0))
    return pl.pallas_call(
        finish_kernel,
        grid=(1,),
        in_specs=[vmem, vmem, vmem, vmem, tail],
        out_specs=[vmem, tail],
        out_shape=[
            jax.ShapeDtypeStruct(gain.shape, jnp.float32),
            jax.ShapeDtypeStruct(payload.shape, payload.dtype),
        ],
        input_output_aliases={4: 1},
        compiler_params=pltpu.CompilerParams(vmem_limit_bytes=VMEM_LIMIT),
        cost_estimate=pl.CostEstimate(flops=2**20, bytes_accessed=2**20, transcendentals=0),
    )(blocks, lines, gain, zeros, payload)


def hidden_kernel(even_ref, received, order_ref, hidden_ref, moments_ref):
    f32, bf16 = jnp.float32, jnp.bfloat16
    tokens = order_ref.shape[0]
    summed = jnp.sum(received[...], axis=0)
    extra = summed[tokens:]
    moments_ref[...] = extra
    mean = extra[2:3] / D
    scale = lax.rsqrt(extra[3:4] / D - mean * mean + epsilon)
    columns = jnp.concatenate((scale, mean, jnp.zeros((tokens - 2, tokens), f32)), axis=0).T
    product = summed[:tokens]
    preact = columns[:, :1] * (product - columns[:, 1:2] * extra[:1]) + extra[1:2]
    gelu = jax.nn.gelu(preact, approximate=True)
    hidden = jnp.where(even_ref[0] == 1, gelu, product).astype(bf16)
    hidden = jnp.dot(order_ref[...], hidden, preferred_element_type=f32).astype(bf16)
    for i in range(hidden_ref.shape[0]):
        hidden_ref[i] = hidden


def late_kernel(even_ref, moments_ref, term_ref, lines_ref, gain_ref, late_ref):
    f32 = jnp.float32
    term = term_ref[...]
    saved, stream, gradient = (lines_ref[i].astype(f32) for i in range(3))
    token_of = lax.broadcasted_iota(jnp.int32, saved.shape, 0) % 2
    saved_total, saved_squares, scaled_total, scaled_saved = (
        jnp.where(token_of == 0, moments_ref[4:5, i : i + 1], moments_ref[4:5, i + 1 : i + 2])
        for i in range(0, 8, 2)
    )
    saved_mean = saved_total / D
    saved_scale = lax.rsqrt(saved_squares / D - saved_mean * saved_mean + epsilon)
    first_mean = scaled_total / D
    second_mean = saved_scale * (scaled_saved / D - saved_mean * first_mean)
    saved_hat = (saved - saved_mean) * saved_scale
    change = saved_scale * (term * gain_ref[...] - first_mean - saved_hat * second_mean)
    late = jnp.where(even_ref[0] == 1, gradient + change, stream + term)
    late_ref[...] = late.astype(jnp.bfloat16)


def assemble_kernel(half_ref, *refs):
    blocks, hidden_ref = refs[:-1], refs[-1]
    cols = len(blocks)
    for i in range(cols):
        hidden_ref[:, i * 128 : i * 128 + 128] = blocks[i][0]


def assemble_call(half, incoming):
    cols, (tokens, part) = incoming.shape[0] // 2, incoming.shape[1:]

    def block(i):
        return pl.BlockSpec((1, tokens, part), lambda k, half: ((1 - half[0]) * cols + i, 0, 0))

    return pl.pallas_call(
        assemble_kernel,
        grid_spec=pltpu.PrefetchScalarGridSpec(
            num_scalar_prefetch=1,
            grid=(1,),
            in_specs=[block(i) for i in range(cols)],
            out_specs=pl.BlockSpec((tokens, cols * part), lambda k, half: (0, 0)),
        ),
        out_shape=jax.ShapeDtypeStruct((tokens, cols * part), incoming.dtype),
        compiler_params=pltpu.CompilerParams(vmem_limit_bytes=VMEM_LIMIT),
        cost_estimate=pl.CostEstimate(flops=2**35, bytes_accessed=2**26, transcendentals=0),
    )(half.astype(jnp.int32).reshape(1), *[incoming] * cols)


def vmem_call(kernel, flag, out_shape, cost, *operands):
    vmem = pl.BlockSpec(memory_space=pltpu.VMEM)
    return pl.pallas_call(
        kernel,
        in_specs=[pl.BlockSpec(memory_space=pltpu.SMEM)] + [vmem] * len(operands),
        out_specs=[vmem] * len(out_shape),
        out_shape=out_shape,
        compiler_params=pltpu.CompilerParams(vmem_limit_bytes=VMEM_LIMIT),
        cost_estimate=pl.CostEstimate(flops=cost, bytes_accessed=cost, transcendentals=0),
    )(flag, *operands)


def per_device(act_in, hid_in, grad_in, saved_in, saved_pre, weights, norm_gain, norm_bias):
    f32, bf16 = jnp.float32, jnp.bfloat16
    half = lax.axis_index(HALF)
    core = lax.axis_index(CORE)
    layer = lax.axis_index(LAYER_AXIS)
    is_even = half == 0
    gain = lax.dynamic_index_in_dim(norm_gain, layer, 0, keepdims=False)
    offset_bias = lax.dynamic_index_in_dim(norm_bias, layer, 0, keepdims=False)
    weight = weights[0]
    stream, gradient = act_in[0], grad_in[0]
    features, hidden = weight.shape
    tokens = hid_in.shape[1]
    own = stream.shape[0]
    nx, ny, cols = lax.axis_size(PX), lax.axis_size(PY), lax.axis_size(COLS)
    half_tokens = tokens // 2
    part = hidden // cols

    early = jnp.where(is_even, *lax.optimization_barrier((stream, gradient)))
    early = lax.ppermute(early, SECTION, [(0, 1), (1, 0), (2, 3), (3, 2)])

    leading = copies(jnp.where(is_even, stream, gradient), PLANE)

    token = jnp.arange(tokens)
    t_of = token % own
    slope = gelu_slope(saved_pre[0].astype(f32), hid_in[0].astype(f32)).astype(bf16)
    right_side = jnp.where(is_even, slope, hid_in[0])
    row, group = token % half_tokens, token // half_tokens
    right_side = picked(right_side, (row // own * 2 + (group != core)) * own + row % own)
    near = exchange(leading, PLANE)
    cores = [(0, 1), (1, 0)]
    own_terms, other_terms = terms_call(right_side, weight)
    arriving = lax.ppermute(other_terms, CORE, cores)
    chip_terms = add_call(own_terms, arriving, zero_after(near))
    near, chip_terms = lax.optimization_barrier((near, chip_terms))
    term_blocks = exchange(chip_terms, PLANE)

    near = near.reshape(half_tokens, features)
    far = lax.ppermute(near, CORE, cores)
    factor = jnp.where(is_even, gain, 1.0)
    vectors = jnp.concatenate(
        (factor[None], offset_bias[None], jnp.zeros((6, features), f32))
    )
    near_parts = rows_call(near_kernel, [near], vectors, weight)
    payload = rows_call(far_kernel, [far], vectors, weight, near_parts)

    line_gain = lines_of(jnp.broadcast_to(gain[None], (own, features)))[0]
    lines = lines_of(jnp.stack((saved_in[0], stream, gradient)))
    term, payload = finish_call(
        term_blocks, lines, line_gain, zero_after(term_blocks), payload
    )
    other = ((token // own) % 2 != core).astype(jnp.int32)
    x_of = token // (2 * own * ny)
    place = ((other * nx + x_of) * ny + (token // (2 * own)) % ny) * own + t_of
    order = (place[:, None] == token[None, :]).astype(bf16)
    payload, early = lax.optimization_barrier((payload, early))
    received = exchange(payload, COLS)
    flag = is_even.astype(jnp.int32).reshape(1)
    hidden_value, moments = vmem_call(
        hidden_kernel,
        flag,
        [
            jax.ShapeDtypeStruct((2 * cols, tokens, part), bf16),
            jax.ShapeDtypeStruct((8, part), f32),
        ],
        0,
        received,
        order,
    )
    (late,) = vmem_call(
        late_kernel,
        flag,
        [jax.ShapeDtypeStruct(term.shape, bf16)],
        2**24,
        moments,
        term,
        lines,
        line_gain,
    )

    incoming = exchange(hidden_value, (HALF, COLS))
    hidden_next = assemble_call(half, incoming)

    late = lax.ppermute(late, SECTION, [(0, 3), (3, 0), (1, 2), (2, 1)])
    late = late.reshape(8, own, 4, 128).transpose(1, 2, 0, 3).reshape(own, features)

    late, hidden_next = lax.optimization_barrier((late, hidden_next))
    act_next = jnp.where(is_even, late, early)
    grad_next = jnp.where(is_even, early, late)
    return (act_next[None], hidden_next[None], grad_next[None])


def solution(mesh):
    names = SECTION + ROWS + (COLS,)
    parts = Mesh(mesh.devices.reshape(2, 2, 4, 8, 2, 3), names)
    in_specs = (
        P(SECTION, ROWS, COLS),
        P(SECTION, None, ROWS),
        P(SECTION, ROWS, COLS),
        P(SECTION, ROWS, COLS),
        P(SECTION, None, ROWS),
        P(SECTION, COLS, ROWS),
        P(None, COLS),
        P(None, COLS),
    )
    out_specs = (P(SECTION, ROWS, COLS), P(SECTION, None, ROWS), P(SECTION, ROWS, COLS))
    return jax.shard_map(
        per_device, mesh=parts, in_specs=in_specs, out_specs=out_specs, check_vma=False
    )
```

```python
import jax
import jax.numpy as jnp
from jax import lax
from jax.experimental import pallas as pl
from jax.experimental.pallas import tpu as pltpu
from jax.sharding import Mesh, PartitionSpec as P

D = 12288
epsilon = 1e-05

LAYER_AXIS, HALF, COLS = "layer", "half", "cols"
PX, PY = "px", "py"
CORE = "core"
PLANE = (PX, PY)
ROWS = PLANE + (CORE,)
SECTION = (LAYER_AXIS, HALF)


def gelu_slope(preact, upstream):
    return jax.vjp(lambda value: jax.nn.gelu(value, approximate=True), preact)[1](upstream)[0]


def exchange(blocks, axis):
    return lax.all_to_all(blocks, axis, 0, 0, tiled=True)


def copies(block, axis):
    return jnp.broadcast_to(block[None], (lax.axis_size(axis), *block.shape))


def picked(rows, index):
    one_hot = (index[:, None] == jnp.arange(rows.shape[0])[None, :]).astype(rows.dtype)
    return jnp.dot(one_hot, rows, preferred_element_type=jnp.float32).astype(rows.dtype)


def high_low(values):
    high = values.astype(jnp.bfloat16)
    return high, (values - high.astype(jnp.float32)).astype(jnp.bfloat16)


def lane_groups(values):
    return sum(values[:, i : i + 128] for i in range(0, values.shape[1], 128))


def rows_step(rows, vectors_ref, weight_ref, result_ref):
    count = rows.shape[0]

    @pl.when(pl.program_id(0) == 0)
    def _():
        result_ref[...] = jnp.zeros_like(result_ref)

    floats = rows.astype(jnp.float32)
    vectors = vectors_ref[...]
    pieces = high_low(floats * vectors[:1]) + high_low(vectors)
    left = jnp.concatenate(pieces, axis=0)
    result = jnp.dot(left, weight_ref[...], preferred_element_type=jnp.float32)
    more = result[2 * count :]
    result_ref[:count] += result[:count] + result[count : 2 * count]
    result_ref[count : count + 8] += more[:8] + more[8:]
    result_ref[count + 8 :, :128] += lane_groups(floats)
    result_ref[count + 8 :, 128:256] += lane_groups(floats * floats)


def near_kernel(rows_ref, vectors_ref, weight_ref, result_ref):
    rows_step(rows_ref[...], vectors_ref, weight_ref, result_ref)


def far_kernel(rows_ref, vectors_ref, weight_ref, near_ref, payload, result_ref):
    rows_step(rows_ref[...], vectors_ref, weight_ref, result_ref)

    @pl.when(pl.program_id(0) == pl.num_programs(0) - 1)
    def _():
        count = rows_ref.shape[0]
        both = jnp.concatenate((near_ref[count + 8 :, :256], result_ref[count + 8 :, :256]), axis=0)
        totals = [
            jnp.sum(both[:, i : i + 128].T, axis=0, keepdims=True) for i in (0, 128)
        ] + [jnp.zeros((4, 128), jnp.float32)]
        for i in range(payload.shape[0]):
            part = slice(i * 128, (i + 1) * 128)
            payload[i, :count] = near_ref[:count, part]
            payload[i, count : 2 * count] = result_ref[:count, part]
            payload[i, 2 * count :] = jnp.concatenate(
                [near_ref[count : count + 2, part]] + totals, axis=0
            )


STEPS = 4
VMEM_LIMIT = 12 * 2**20


def rows_call(kernel, blocks, vectors, weight, near=None):
    count = sum(block.shape[0] for block in blocks)
    features, hidden = weight.shape
    step = features // STEPS
    f32 = jnp.float32
    shape = (2 * count + 8, hidden)
    whole = pl.BlockSpec(shape, lambda k: (0, 0))
    specs = [pl.BlockSpec((block.shape[0], step), lambda k: (0, k)) for block in blocks] + [
        pl.BlockSpec((8, step), lambda k: (0, k)),
        pl.BlockSpec((step, hidden), lambda k: (k, 0)),
    ]
    if near is None:
        out_shape, out_specs = jax.ShapeDtypeStruct(shape, f32), whole
        scratch, near = [], ()
    else:
        out = (hidden // 128, 2 * count + 8, 128)
        out_shape = jax.ShapeDtypeStruct(out, f32)
        out_specs = pl.BlockSpec(out, lambda k: (0, 0, 0))
        specs = specs + [whole]
        scratch, near = [pltpu.VMEM(shape, f32)], (near,)
    return pl.pallas_call(
        kernel,
        grid=(STEPS,),
        in_specs=specs,
        out_specs=out_specs,
        out_shape=out_shape,
        scratch_shapes=scratch,
        compiler_params=pltpu.CompilerParams(vmem_limit_bytes=VMEM_LIMIT),
        cost_estimate=pl.CostEstimate(flops=0, bytes_accessed=0, transcendentals=0),
    )(*blocks, vectors, weight, *near)


def blocks_of(values):
    row = lax.broadcasted_iota(jnp.int32, (8, 128), 0) // 2
    blocks = []
    for low in range(0, values.shape[0], 8):
        tiles = [values[low : low + 8, m * 128 : m * 128 + 128] for m in range(8)]
        for i in range(4):
            halves = []
            for first in (0, 4):
                half = jnp.zeros((8, 128), jnp.float32)
                for m in range(4):
                    moved = pltpu.roll(tiles[first + m], (2 * (m - i)) % 8, 0)
                    half = jnp.where(row == m, moved, half)
                halves.append(half)
            blocks.append(jnp.concatenate(halves, axis=0))
    return blocks


def terms_kernel(rows_ref, weight_ref, own_ref, other_ref):
    values = lax.dot_general(
        rows_ref[...],
        weight_ref[...],
        (((1,), (1,)), ((), ())),
        preferred_element_type=jnp.float32,
    )
    half = values.shape[0] // 2
    for p, block in enumerate(blocks_of(values[half:])):
        other_ref[p] = block.astype(jnp.bfloat16)
    for p, block in enumerate(blocks_of(values[:half])):
        own_ref[p] = block


def terms_call(rows, weight):
    count, hidden = rows.shape
    features = weight.shape[0]
    block = pl.BlockSpec((count // 4, 16, 128), lambda k: (0, 0, k))
    shape = (count // 4, 16, features // 8)
    return pl.pallas_call(
        terms_kernel,
        grid=(features // 1024,),
        in_specs=[
            pl.BlockSpec((count, hidden), lambda k: (0, 0)),
            pl.BlockSpec((1024, hidden), lambda k: (k, 0)),
        ],
        out_specs=[block, block],
        out_shape=[
            pltpu.HBM(shape, jnp.float32),
            pltpu.HBM(shape, jnp.bfloat16),
        ],
        compiler_params=pltpu.CompilerParams(vmem_limit_bytes=VMEM_LIMIT),
        cost_estimate=pl.CostEstimate(flops=0, bytes_accessed=0, transcendentals=0),
    )(rows, weight)


def zero_kernel(anything_ref, zero_ref):
    zero_ref[...] = jnp.zeros_like(zero_ref)


def zero_after(anything):
    return pl.pallas_call(
        zero_kernel,
        in_specs=[pl.BlockSpec(memory_space=pl.ANY)],
        out_specs=pl.BlockSpec(memory_space=pltpu.VMEM),
        out_shape=jax.ShapeDtypeStruct((8, 128), jnp.float32),
        compiler_params=pltpu.CompilerParams(vmem_limit_bytes=2**20),
        cost_estimate=pl.CostEstimate(flops=2**35, bytes_accessed=2**26, transcendentals=0),
    )(anything)


def add_kernel(own_ref, arriving_ref, zero_ref, sum_ref):
    values = own_ref[...] + arriving_ref[...].astype(jnp.float32)
    sum_ref[...] = (values + zero_ref[0, 0]).astype(jnp.bfloat16)


def add_call(own, arriving, zeros):
    block = pl.BlockSpec((own.shape[0] // 2, *own.shape[1:]), lambda k: (k, 0, 0))
    return pl.pallas_call(
        add_kernel,
        grid=(2,),
        in_specs=[block, block, pl.BlockSpec(zeros.shape, lambda k: (0, 0))],
        out_specs=block,
        out_shape=pltpu.HBM(own.shape, jnp.bfloat16),
        compiler_params=pltpu.CompilerParams(vmem_limit_bytes=VMEM_LIMIT),
        cost_estimate=pl.CostEstimate(flops=0, bytes_accessed=0, transcendentals=0),
    )(pltpu.with_memory_space_constraint(own, pltpu.HBM), arriving, zeros)


def lines_of(values):
    values = values.reshape(-1, 2, 4, 8, 128).transpose(0, 3, 1, 2, 4)
    return values.reshape(-1, 16, 512)


def total(values):
    return jnp.sum(jnp.sum(values, axis=0, keepdims=True), axis=1, keepdims=True)


def finish_kernel(blocks, lines_ref, gain_ref, zero_ref, payload_in, term_ref, payload_out):
    term = jnp.sum(blocks[...].astype(jnp.float32), axis=0) + zero_ref[0, 0]
    term_ref[...] = term
    saved = lines_ref[0].astype(jnp.float32)
    scaled = term * gain_ref[...]
    lane = lax.broadcasted_iota(jnp.int32, (1, 128), 1)
    token_of = lax.broadcasted_iota(jnp.int32, saved.shape, 0) % 2
    moments = jnp.zeros((1, 128), jnp.float32)
    for i, values in enumerate((saved, saved * saved, scaled, scaled * saved)):
        for token in range(2):
            part = total(jnp.where(token_of == token, values, 0.0))
            moments = jnp.where(lane == 2 * i + token, part, moments)
    row = lax.broadcasted_iota(jnp.int32, (8, 128), 0)
    for i in range(payload_out.shape[0]):
        payload_out[i] = jnp.where(row == 4, moments, payload_in[i])


def finish_call(blocks, lines, gain, zeros, payload):
    vmem = pl.BlockSpec(memory_space=pltpu.VMEM)
    tail = pl.BlockSpec((payload.shape[0], 8, 128), lambda i: (0, payload.shape[1] // 8 - 1, 0))
    return pl.pallas_call(
        finish_kernel,
        grid=(1,),
        in_specs=[vmem, vmem, vmem, vmem, tail],
        out_specs=[vmem, tail],
        out_shape=[
            jax.ShapeDtypeStruct(gain.shape, jnp.float32),
            jax.ShapeDtypeStruct(payload.shape, payload.dtype),
        ],
        input_output_aliases={4: 1},
        compiler_params=pltpu.CompilerParams(vmem_limit_bytes=VMEM_LIMIT),
        cost_estimate=pl.CostEstimate(flops=2**20, bytes_accessed=2**20, transcendentals=0),
    )(blocks, lines, gain, zeros, payload)


def hidden_kernel(even_ref, received, order_ref, hidden_ref, moments_ref):
    f32, bf16 = jnp.float32, jnp.bfloat16
    tokens = order_ref.shape[0]
    summed = jnp.sum(received[...], axis=0)
    extra = summed[tokens:]
    moments_ref[...] = extra
    mean = extra[2:3] / D
    scale = lax.rsqrt(extra[3:4] / D - mean * mean + epsilon)
    columns = jnp.concatenate((scale, mean, jnp.zeros((tokens - 2, tokens), f32)), axis=0).T
    product = summed[:tokens]
    preact = columns[:, :1] * (product - columns[:, 1:2] * extra[:1]) + extra[1:2]
    gelu = jax.nn.gelu(preact, approximate=True)
    hidden = jnp.where(even_ref[0] == 1, gelu, product).astype(bf16)
    hidden = jnp.dot(order_ref[...], hidden, preferred_element_type=f32).astype(bf16)
    for i in range(hidden_ref.shape[0]):
        hidden_ref[i] = hidden


def late_kernel(even_ref, moments_ref, term_ref, lines_ref, gain_ref, late_ref):
    f32 = jnp.float32
    term = term_ref[...]
    saved, stream, gradient = (lines_ref[i].astype(f32) for i in range(3))
    token_of = lax.broadcasted_iota(jnp.int32, saved.shape, 0) % 2
    saved_total, saved_squares, scaled_total, scaled_saved = (
        jnp.where(token_of == 0, moments_ref[4:5, i : i + 1], moments_ref[4:5, i + 1 : i + 2])
        for i in range(0, 8, 2)
    )
    saved_mean = saved_total / D
    saved_scale = lax.rsqrt(saved_squares / D - saved_mean * saved_mean + epsilon)
    first_mean = scaled_total / D
    second_mean = saved_scale * (scaled_saved / D - saved_mean * first_mean)
    saved_hat = (saved - saved_mean) * saved_scale
    change = saved_scale * (term * gain_ref[...] - first_mean - saved_hat * second_mean)
    late = jnp.where(even_ref[0] == 1, gradient + change, stream + term)
    late_ref[...] = late.astype(jnp.bfloat16)


def assemble_kernel(half_ref, *refs):
    blocks, hidden_ref = refs[:-1], refs[-1]
    cols = len(blocks)
    for i in range(cols):
        hidden_ref[:, i * 128 : i * 128 + 128] = blocks[i][0]


def assemble_call(half, incoming):
    cols, (tokens, part) = incoming.shape[0] // 2, incoming.shape[1:]

    def block(i):
        return pl.BlockSpec((1, tokens, part), lambda k, half: ((1 - half[0]) * cols + i, 0, 0))

    return pl.pallas_call(
        assemble_kernel,
        grid_spec=pltpu.PrefetchScalarGridSpec(
            num_scalar_prefetch=1,
            grid=(1,),
            in_specs=[block(i) for i in range(cols)],
            out_specs=pl.BlockSpec((tokens, cols * part), lambda k, half: (0, 0)),
        ),
        out_shape=jax.ShapeDtypeStruct((tokens, cols * part), incoming.dtype),
        compiler_params=pltpu.CompilerParams(vmem_limit_bytes=VMEM_LIMIT),
        cost_estimate=pl.CostEstimate(flops=2**35, bytes_accessed=2**26, transcendentals=0),
    )(half.astype(jnp.int32).reshape(1), *[incoming] * cols)


def vmem_call(kernel, flag, out_shape, cost, *operands):
    vmem = pl.BlockSpec(memory_space=pltpu.VMEM)
    return pl.pallas_call(
        kernel,
        in_specs=[pl.BlockSpec(memory_space=pltpu.SMEM)] + [vmem] * len(operands),
        out_specs=[vmem] * len(out_shape),
        out_shape=out_shape,
        compiler_params=pltpu.CompilerParams(vmem_limit_bytes=VMEM_LIMIT),
        cost_estimate=pl.CostEstimate(flops=cost, bytes_accessed=cost, transcendentals=0),
    )(flag, *operands)


def per_device(act_in, hid_in, grad_in, saved_in, saved_pre, weights, norm_gain, norm_bias):
    f32, bf16 = jnp.float32, jnp.bfloat16
    half = lax.axis_index(HALF)
    core = lax.axis_index(CORE)
    layer = lax.axis_index(LAYER_AXIS)
    is_even = half == 0
    gain = lax.dynamic_index_in_dim(norm_gain, layer, 0, keepdims=False)
    offset_bias = lax.dynamic_index_in_dim(norm_bias, layer, 0, keepdims=False)
    weight = weights[0]
    stream, gradient = act_in[0], grad_in[0]
    features, hidden = weight.shape
    tokens = hid_in.shape[1]
    own = stream.shape[0]
    nx, ny, cols = lax.axis_size(PX), lax.axis_size(PY), lax.axis_size(COLS)
    half_tokens = tokens // 2
    part = hidden // cols

    early = jnp.where(is_even, *lax.optimization_barrier((stream, gradient)))
    early = lax.ppermute(early, SECTION, [(0, 1), (1, 0), (2, 3), (3, 2)])

    leading = jnp.where(is_even, copies(stream, PLANE), copies(gradient, PLANE))

    token = jnp.arange(tokens)
    t_of = token % own
    slope = gelu_slope(saved_pre[0].astype(f32), hid_in[0].astype(f32)).astype(bf16)
    right_side = jnp.where(is_even, slope, hid_in[0])
    row, group = token % half_tokens, token // half_tokens
    right_side = picked(right_side, (row // own * 2 + (group != core)) * own + row % own)
    near = exchange(leading, PLANE)
    cores = [(0, 1), (1, 0)]
    own_terms, other_terms = terms_call(right_side, weight)
    arriving = lax.ppermute(other_terms, CORE, cores)
    chip_terms = add_call(own_terms, arriving, zero_after(near[0, :, :128]))
    near, chip_terms = lax.optimization_barrier((near, chip_terms))
    term_blocks = exchange(chip_terms, PLANE)

    near = near.reshape(half_tokens, features)
    far = lax.ppermute(near, CORE, cores)
    factor = jnp.where(is_even, gain, 1.0)
    vectors = jnp.concatenate(
        (factor[None], offset_bias[None], jnp.zeros((6, features), f32))
    )
    near_parts = rows_call(near_kernel, [near], vectors, weight)
    payload = rows_call(far_kernel, [far], vectors, weight, near_parts)

    line_gain = lines_of(jnp.broadcast_to(gain[None], (own, features)))[0]
    lines = lines_of(jnp.stack((saved_in[0], stream, gradient)))
    term, payload = finish_call(
        term_blocks, lines, line_gain, zero_after(term_blocks), payload
    )
    other = ((token // own) % 2 != core).astype(jnp.int32)
    x_of = token // (2 * own * ny)
    place = ((other * nx + x_of) * ny + (token // (2 * own)) % ny) * own + t_of
    order = (place[:, None] == token[None, :]).astype(bf16)
    payload, early = lax.optimization_barrier((payload, early))
    received = exchange(payload, COLS)
    flag = is_even.astype(jnp.int32).reshape(1)
    hidden_value, moments = vmem_call(
        hidden_kernel,
        flag,
        [
            jax.ShapeDtypeStruct((2 * cols, tokens, part), bf16),
            jax.ShapeDtypeStruct((8, part), f32),
        ],
        0,
        received,
        order,
    )
    (late,) = vmem_call(
        late_kernel,
        flag,
        [jax.ShapeDtypeStruct(term.shape, bf16)],
        2**24,
        moments,
        term,
        lines,
        line_gain,
    )

    incoming = exchange(hidden_value, (HALF, COLS))
    hidden_next = assemble_call(half, incoming)

    late = lax.ppermute(late, SECTION, [(0, 3), (3, 0), (1, 2), (2, 1)])
    late = late.reshape(8, own, 4, 128).transpose(1, 2, 0, 3).reshape(own, features)

    late, hidden_next = lax.optimization_barrier((late, hidden_next))
    act_next = jnp.where(is_even, late, early)
    grad_next = jnp.where(is_even, early, late)
    return (act_next[None], hidden_next[None], grad_next[None])


def solution(mesh):
    names = SECTION + ROWS + (COLS,)
    parts = Mesh(mesh.devices.reshape(2, 2, 4, 8, 2, 3), names)
    in_specs = (
        P(SECTION, ROWS, COLS),
        P(SECTION, None, ROWS),
        P(SECTION, ROWS, COLS),
        P(SECTION, ROWS, COLS),
        P(SECTION, None, ROWS),
        P(SECTION, COLS, ROWS),
        P(None, COLS),
        P(None, COLS),
    )
    out_specs = (P(SECTION, ROWS, COLS), P(SECTION, None, ROWS), P(SECTION, ROWS, COLS))
    return jax.shard_map(
        per_device, mesh=parts, in_specs=in_specs, out_specs=out_specs, check_vma=False
    )
```

```python
import jax
import jax.numpy as jnp
from jax import lax
from jax.experimental import pallas as pl
from jax.experimental.pallas import tpu as pltpu
from jax.sharding import Mesh, PartitionSpec as P

D = 12288
epsilon = 1e-05

LAYER_AXIS, HALF, COLS = "layer", "half", "cols"
PX, PY = "px", "py"
CORE = "core"
PLANE = (PX, PY)
ROWS = PLANE + (CORE,)
SECTION = (LAYER_AXIS, HALF)


def gelu_slope(preact, upstream):
    return jax.vjp(lambda value: jax.nn.gelu(value, approximate=True), preact)[1](upstream)[0]


def exchange(blocks, axis):
    return lax.all_to_all(blocks, axis, 0, 0, tiled=True)


def copies(block, axis):
    return jnp.broadcast_to(block[None], (lax.axis_size(axis), *block.shape))


def picked(rows, index):
    one_hot = (index[:, None] == jnp.arange(rows.shape[0])[None, :]).astype(rows.dtype)
    return jnp.dot(one_hot, rows, preferred_element_type=jnp.float32).astype(rows.dtype)


def high_low(values):
    high = values.astype(jnp.bfloat16)
    return high, (values - high.astype(jnp.float32)).astype(jnp.bfloat16)


def lane_groups(values):
    return sum(values[:, i : i + 128] for i in range(0, values.shape[1], 128))


def rows_step(rows, vectors_ref, weight_ref, result_ref):
    count = rows.shape[0]

    @pl.when(pl.program_id(0) == 0)
    def _():
        result_ref[...] = jnp.zeros_like(result_ref)

    floats = rows.astype(jnp.float32)
    vectors = vectors_ref[...]
    pieces = high_low(floats * vectors[:1]) + high_low(vectors)
    left = jnp.concatenate(pieces, axis=0)
    result = jnp.dot(left, weight_ref[...], preferred_element_type=jnp.float32)
    more = result[2 * count :]
    result_ref[:count] += result[:count] + result[count : 2 * count]
    result_ref[count : count + 8] += more[:8] + more[8:]
    result_ref[count + 8 :, :128] += lane_groups(floats)
    result_ref[count + 8 :, 128:256] += lane_groups(floats * floats)


def near_kernel(rows_ref, vectors_ref, weight_ref, result_ref):
    rows_step(rows_ref[...], vectors_ref, weight_ref, result_ref)


def far_kernel(rows_ref, vectors_ref, weight_ref, near_ref, payload, result_ref):
    rows_step(rows_ref[...], vectors_ref, weight_ref, result_ref)

    @pl.when(pl.program_id(0) == pl.num_programs(0) - 1)
    def _():
        count = rows_ref.shape[0]
        both = jnp.concatenate((near_ref[count + 8 :, :256], result_ref[count + 8 :, :256]), axis=0)
        totals = [
            jnp.sum(both[:, i : i + 128].T, axis=0, keepdims=True) for i in (0, 128)
        ] + [jnp.zeros((4, 128), jnp.float32)]
        for i in range(payload.shape[0]):
            part = slice(i * 128, (i + 1) * 128)
            payload[i, :count] = near_ref[:count, part]
            payload[i, count : 2 * count] = result_ref[:count, part]
            payload[i, 2 * count :] = jnp.concatenate(
                [near_ref[count : count + 2, part]] + totals, axis=0
            )


STEPS = 4
VMEM_LIMIT = 12 * 2**20


def rows_call(kernel, blocks, vectors, weight, near=None):
    count = sum(block.shape[0] for block in blocks)
    features, hidden = weight.shape
    step = features // STEPS
    f32 = jnp.float32
    shape = (2 * count + 8, hidden)
    whole = pl.BlockSpec(shape, lambda k: (0, 0))
    specs = [pl.BlockSpec((block.shape[0], step), lambda k: (0, k)) for block in blocks] + [
        pl.BlockSpec((8, step), lambda k: (0, k)),
        pl.BlockSpec((step, hidden), lambda k: (k, 0)),
    ]
    if near is None:
        out_shape, out_specs = jax.ShapeDtypeStruct(shape, f32), whole
        scratch, near = [], ()
    else:
        out = (hidden // 128, 2 * count + 8, 128)
        out_shape = jax.ShapeDtypeStruct(out, f32)
        out_specs = pl.BlockSpec(out, lambda k: (0, 0, 0))
        specs = specs + [whole]
        scratch, near = [pltpu.VMEM(shape, f32)], (near,)
    return pl.pallas_call(
        kernel,
        grid=(STEPS,),
        in_specs=specs,
        out_specs=out_specs,
        out_shape=out_shape,
        scratch_shapes=scratch,
        compiler_params=pltpu.CompilerParams(vmem_limit_bytes=VMEM_LIMIT),
        cost_estimate=pl.CostEstimate(flops=0, bytes_accessed=0, transcendentals=0),
    )(*blocks, vectors, weight, *near)


def blocks_of(values):
    row = lax.broadcasted_iota(jnp.int32, (8, 128), 0) // 2
    blocks = []
    for low in range(0, values.shape[0], 8):
        tiles = [values[low : low + 8, m * 128 : m * 128 + 128] for m in range(8)]
        for i in range(4):
            halves = []
            for first in (0, 4):
                half = jnp.zeros((8, 128), jnp.float32)
                for m in range(4):
                    moved = pltpu.roll(tiles[first + m], (2 * (m - i)) % 8, 0)
                    half = jnp.where(row == m, moved, half)
                halves.append(half)
            blocks.append(jnp.concatenate(halves, axis=0))
    return blocks


def terms_kernel(rows_ref, weight_ref, own_ref, other_ref):
    values = lax.dot_general(
        rows_ref[...],
        weight_ref[...],
        (((1,), (1,)), ((), ())),
        preferred_element_type=jnp.float32,
    )
    half = values.shape[0] // 2
    for p, block in enumerate(blocks_of(values[half:])):
        other_ref[p] = block.astype(jnp.bfloat16)
    for p, block in enumerate(blocks_of(values[:half])):
        own_ref[p] = block


def terms_call(rows, weight):
    count, hidden = rows.shape
    features = weight.shape[0]
    block = pl.BlockSpec((count // 4, 16, 128), lambda k: (0, 0, k))
    shape = (count // 4, 16, features // 8)
    return pl.pallas_call(
        terms_kernel,
        grid=(features // 1024,),
        in_specs=[
            pl.BlockSpec((count, hidden), lambda k: (0, 0)),
            pl.BlockSpec((1024, hidden), lambda k: (k, 0)),
        ],
        out_specs=[block, block],
        out_shape=[
            pltpu.HBM(shape, jnp.float32),
            pltpu.HBM(shape, jnp.bfloat16),
        ],
        compiler_params=pltpu.CompilerParams(vmem_limit_bytes=VMEM_LIMIT),
        cost_estimate=pl.CostEstimate(flops=0, bytes_accessed=0, transcendentals=0),
    )(rows, weight)


def zero_kernel(anything_ref, zero_ref):
    zero_ref[...] = jnp.zeros_like(zero_ref)


def zero_after(anything):
    return pl.pallas_call(
        zero_kernel,
        in_specs=[pl.BlockSpec(memory_space=pl.ANY)],
        out_specs=pl.BlockSpec(memory_space=pltpu.VMEM),
        out_shape=jax.ShapeDtypeStruct((8, 128), jnp.float32),
        compiler_params=pltpu.CompilerParams(vmem_limit_bytes=2**20),
        cost_estimate=pl.CostEstimate(flops=2**35, bytes_accessed=2**26, transcendentals=0),
    )(anything)


def add_kernel(own_ref, arriving_ref, zero_ref, sum_ref):
    values = own_ref[...] + arriving_ref[...].astype(jnp.float32)
    sum_ref[...] = (values + zero_ref[0, 0]).astype(jnp.bfloat16)


def add_call(own, arriving, zeros):
    block = pl.BlockSpec((own.shape[0] // 2, *own.shape[1:]), lambda k: (k, 0, 0))
    return pl.pallas_call(
        add_kernel,
        grid=(2,),
        in_specs=[block, block, pl.BlockSpec(zeros.shape, lambda k: (0, 0))],
        out_specs=block,
        out_shape=pltpu.HBM(own.shape, jnp.bfloat16),
        compiler_params=pltpu.CompilerParams(vmem_limit_bytes=VMEM_LIMIT),
        cost_estimate=pl.CostEstimate(flops=0, bytes_accessed=0, transcendentals=0),
    )(pltpu.with_memory_space_constraint(own, pltpu.HBM), arriving, zeros)


def lines_of(values):
    values = values.reshape(-1, 2, 4, 8, 128).transpose(0, 3, 1, 2, 4)
    return values.reshape(-1, 16, 512)


def total(values):
    return jnp.sum(jnp.sum(values, axis=0, keepdims=True), axis=1, keepdims=True)


def finish_kernel(blocks, lines_ref, gain_ref, zero_ref, payload_in, term_ref, payload_out):
    term = jnp.sum(blocks[...].astype(jnp.float32), axis=0) + zero_ref[0, 0]
    term_ref[...] = term
    saved = lines_ref[0].astype(jnp.float32)
    scaled = term * gain_ref[...]
    lane = lax.broadcasted_iota(jnp.int32, (1, 128), 1)
    token_of = lax.broadcasted_iota(jnp.int32, saved.shape, 0) % 2
    moments = jnp.zeros((1, 128), jnp.float32)
    for i, values in enumerate((saved, saved * saved, scaled, scaled * saved)):
        for token in range(2):
            part = total(jnp.where(token_of == token, values, 0.0))
            moments = jnp.where(lane == 2 * i + token, part, moments)
    row = lax.broadcasted_iota(jnp.int32, (8, 128), 0)
    for i in range(payload_out.shape[0]):
        payload_out[i] = jnp.where(row == 4, moments, payload_in[i])


def finish_call(blocks, lines, gain, zeros, payload):
    vmem = pl.BlockSpec(memory_space=pltpu.VMEM)
    tail = pl.BlockSpec((payload.shape[0], 8, 128), lambda i: (0, payload.shape[1] // 8 - 1, 0))
    return pl.pallas_call(
        finish_kernel,
        grid=(1,),
        in_specs=[vmem, vmem, vmem, vmem, tail],
        out_specs=[vmem, tail],
        out_shape=[
            jax.ShapeDtypeStruct(gain.shape, jnp.float32),
            jax.ShapeDtypeStruct(payload.shape, payload.dtype),
        ],
        input_output_aliases={4: 1},
        compiler_params=pltpu.CompilerParams(vmem_limit_bytes=VMEM_LIMIT),
        cost_estimate=pl.CostEstimate(flops=2**20, bytes_accessed=2**20, transcendentals=0),
    )(blocks, lines, gain, zeros, payload)


def hidden_kernel(even_ref, received, order_ref, hidden_ref, moments_ref):
    f32, bf16 = jnp.float32, jnp.bfloat16
    tokens = order_ref.shape[0]
    summed = jnp.sum(received[...], axis=0)
    extra = summed[tokens:]
    moments_ref[...] = extra
    mean = extra[2:3] / D
    scale = lax.rsqrt(extra[3:4] / D - mean * mean + epsilon)
    columns = jnp.concatenate((scale, mean, jnp.zeros((tokens - 2, tokens), f32)), axis=0).T
    product = summed[:tokens]
    preact = columns[:, :1] * (product - columns[:, 1:2] * extra[:1]) + extra[1:2]
    gelu = jax.nn.gelu(preact, approximate=True)
    hidden = jnp.where(even_ref[0] == 1, gelu, product).astype(bf16)
    hidden = jnp.dot(order_ref[...], hidden, preferred_element_type=f32).astype(bf16)
    for i in range(hidden_ref.shape[0]):
        hidden_ref[i] = hidden


def late_kernel(even_ref, moments_ref, term_ref, lines_ref, gain_ref, late_ref):
    f32 = jnp.float32
    term = term_ref[...]
    saved, stream, gradient = (lines_ref[i].astype(f32) for i in range(3))
    token_of = lax.broadcasted_iota(jnp.int32, saved.shape, 0) % 2
    saved_total, saved_squares, scaled_total, scaled_saved = (
        jnp.where(token_of == 0, moments_ref[4:5, i : i + 1], moments_ref[4:5, i + 1 : i + 2])
        for i in range(0, 8, 2)
    )
    saved_mean = saved_total / D
    saved_scale = lax.rsqrt(saved_squares / D - saved_mean * saved_mean + epsilon)
    first_mean = scaled_total / D
    second_mean = saved_scale * (scaled_saved / D - saved_mean * first_mean)
    saved_hat = (saved - saved_mean) * saved_scale
    change = saved_scale * (term * gain_ref[...] - first_mean - saved_hat * second_mean)
    late = jnp.where(even_ref[0] == 1, gradient + change, stream + term)
    late_ref[...] = late.astype(jnp.bfloat16)


def assemble_kernel(half_ref, *refs):
    blocks, hidden_ref = refs[:-1], refs[-1]
    cols = len(blocks)
    for i in range(cols):
        hidden_ref[:, i * 128 : i * 128 + 128] = blocks[i][0]


def assemble_call(half, incoming):
    cols, (tokens, part) = incoming.shape[0] // 2, incoming.shape[1:]

    def block(i):
        return pl.BlockSpec((1, tokens, part), lambda k, half: ((1 - half[0]) * cols + i, 0, 0))

    return pl.pallas_call(
        assemble_kernel,
        grid_spec=pltpu.PrefetchScalarGridSpec(
            num_scalar_prefetch=1,
            grid=(1,),
            in_specs=[block(i) for i in range(cols)],
            out_specs=pl.BlockSpec((tokens, cols * part), lambda k, half: (0, 0)),
        ),
        out_shape=jax.ShapeDtypeStruct((tokens, cols * part), incoming.dtype),
        compiler_params=pltpu.CompilerParams(vmem_limit_bytes=VMEM_LIMIT),
        cost_estimate=pl.CostEstimate(flops=2**35, bytes_accessed=2**26, transcendentals=0),
    )(half.astype(jnp.int32).reshape(1), *[incoming] * cols)


def vmem_call(kernel, flag, out_shape, cost, *operands):
    vmem = pl.BlockSpec(memory_space=pltpu.VMEM)
    return pl.pallas_call(
        kernel,
        in_specs=[pl.BlockSpec(memory_space=pltpu.SMEM)] + [vmem] * len(operands),
        out_specs=[vmem] * len(out_shape),
        out_shape=out_shape,
        compiler_params=pltpu.CompilerParams(vmem_limit_bytes=VMEM_LIMIT),
        cost_estimate=pl.CostEstimate(flops=cost, bytes_accessed=cost, transcendentals=0),
    )(flag, *operands)


def per_device(act_in, hid_in, grad_in, saved_in, saved_pre, weights, norm_gain, norm_bias):
    f32, bf16 = jnp.float32, jnp.bfloat16
    half = lax.axis_index(HALF)
    core = lax.axis_index(CORE)
    layer = lax.axis_index(LAYER_AXIS)
    is_even = half == 0
    gain = lax.dynamic_index_in_dim(norm_gain, layer, 0, keepdims=False)
    offset_bias = lax.dynamic_index_in_dim(norm_bias, layer, 0, keepdims=False)
    weight = weights[0]
    stream, gradient = act_in[0], grad_in[0]
    features, hidden = weight.shape
    tokens = hid_in.shape[1]
    own = stream.shape[0]
    nx, ny, cols = lax.axis_size(PX), lax.axis_size(PY), lax.axis_size(COLS)
    half_tokens = tokens // 2
    part = hidden // cols

    early = jnp.where(is_even, *lax.optimization_barrier((stream, gradient)))
    early = lax.ppermute(early, SECTION, [(0, 1), (1, 0), (2, 3), (3, 2)])

    leading = jnp.where(is_even, copies(stream, PLANE), copies(gradient, PLANE))

    token = jnp.arange(tokens)
    t_of = token % own
    slope = gelu_slope(saved_pre[0].astype(f32), hid_in[0].astype(f32)).astype(bf16)
    right_side = jnp.where(is_even, slope, hid_in[0])
    row, group = token % half_tokens, token // half_tokens
    right_side = picked(right_side, (row // own * 2 + (group != core)) * own + row % own)
    near = exchange(leading, PLANE)
    cores = [(0, 1), (1, 0)]
    own_terms, other_terms = terms_call(right_side, weight)
    arriving = lax.ppermute(other_terms, CORE, cores)
    chip_terms = add_call(own_terms, arriving, zero_after(near[0, :, :128]))
    near, chip_terms = lax.optimization_barrier((near, chip_terms))
    term_blocks = exchange(chip_terms, PLANE)
    term_blocks = pltpu.with_memory_space_constraint(term_blocks, pltpu.VMEM)

    near = near.reshape(half_tokens, features)
    far = lax.ppermute(near, CORE, cores)
    factor = jnp.where(is_even, gain, 1.0)
    vectors = jnp.concatenate(
        (factor[None], offset_bias[None], jnp.zeros((6, features), f32))
    )
    near_parts = rows_call(near_kernel, [near], vectors, weight)
    payload = rows_call(far_kernel, [far], vectors, weight, near_parts)

    line_gain = lines_of(jnp.broadcast_to(gain[None], (own, features)))[0]
    lines = lines_of(jnp.stack((saved_in[0], stream, gradient)))
    term, payload = finish_call(
        term_blocks, lines, line_gain, zero_after(term_blocks), payload
    )
    other = ((token // own) % 2 != core).astype(jnp.int32)
    x_of = token // (2 * own * ny)
    place = ((other * nx + x_of) * ny + (token // (2 * own)) % ny) * own + t_of
    order = (place[:, None] == token[None, :]).astype(bf16)
    payload, early = lax.optimization_barrier((payload, early))
    received = exchange(payload, COLS)
    flag = is_even.astype(jnp.int32).reshape(1)
    hidden_value, moments = vmem_call(
        hidden_kernel,
        flag,
        [
            jax.ShapeDtypeStruct((2 * cols, tokens, part), bf16),
            jax.ShapeDtypeStruct((8, part), f32),
        ],
        0,
        received,
        order,
    )
    (late,) = vmem_call(
        late_kernel,
        flag,
        [jax.ShapeDtypeStruct(term.shape, bf16)],
        2**24,
        moments,
        term,
        lines,
        line_gain,
    )

    incoming = exchange(hidden_value, (HALF, COLS))
    hidden_next = assemble_call(half, incoming)

    late = lax.ppermute(late, SECTION, [(0, 3), (3, 0), (1, 2), (2, 1)])
    late = late.reshape(8, own, 4, 128).transpose(1, 2, 0, 3).reshape(own, features)

    late, hidden_next = lax.optimization_barrier((late, hidden_next))
    act_next = jnp.where(is_even, late, early)
    grad_next = jnp.where(is_even, early, late)
    return (act_next[None], hidden_next[None], grad_next[None])


def solution(mesh):
    names = SECTION + ROWS + (COLS,)
    parts = Mesh(mesh.devices.reshape(2, 2, 4, 8, 2, 3), names)
    in_specs = (
        P(SECTION, ROWS, COLS),
        P(SECTION, None, ROWS),
        P(SECTION, ROWS, COLS),
        P(SECTION, ROWS, COLS),
        P(SECTION, None, ROWS),
        P(SECTION, COLS, ROWS),
        P(None, COLS),
        P(None, COLS),
    )
    out_specs = (P(SECTION, ROWS, COLS), P(SECTION, None, ROWS), P(SECTION, ROWS, COLS))
    return jax.shard_map(
        per_device, mesh=parts, in_specs=in_specs, out_specs=out_specs, check_vma=False
    )
```
